32 devices in a mesh: group: 2 (over y), expert: 4 (over z), query: 2 (over x), dp: 2 (over core).
Axes of the slice: x: 2, y: 2, z: 4, core: 2. Of those that a mesh axis runs over, the one named last changes fastest.
Arguments:
- tokens: bfloat16 [4096, 2048], P(('group', 'expert', 'query', 'dp')), parts along dimension 0, may hold values from -6 to 6
- route_ids: int32 [4096, 4], P(('group', 'expert', 'query', 'dp')), parts along dimension 0, may hold values from 0 to 7, all different within a row; in each aligned block of 128 rows (0 to 127, 128 to 255, ...) at most 128 rows name the same one
- gate_values: float32 [4096, 4], P(('group', 'expert', 'query', 'dp')), parts along dimension 0, may hold values from 0.1 to 1
- passage_lengths: int32 [64], P(('group', 'expert', 'query', 'dp')), parts along dimension 0, may hold values from 16 to 64
- gate_weight: bfloat16 [8, 2048, 384], P(('expert', 'query'), None, 'dp'), may hold values from -0.125 to 0.125
- up_weight: bfloat16 [8, 2048, 384], P(('expert', 'query'), None, 'dp'), may hold values from -0.125 to 0.125
- down_weight: bfloat16 [8, 2048, 384], P(('expert', 'query'), None, 'dp'), may hold values from -0.3125 to 0.3125
- proj_weight: bfloat16 [2048, 128], replicated, may hold values from -0.125 to 0.125
- queries: bfloat16 [128, 32, 128], P(('group', 'query')), parts along dimension 0, may hold values from -0.59765625 to 0.59765625
Outputs:
- scores: float32 [64, 64], P(('group', 'expert', 'query', 'dp')), parts along dimension 0
The draws below stay inside these ranges and needn't reach their ends.
There are 2 independent parts, one for each index of `group`. The reference program is written for one: setup_inputs(seed, part) draws one part's arguments, and reference() takes and returns one part's arrays. A program takes and returns all parts, laid end to end along the dimension named above; an argument that names none is the same for every part. Nothing has to cross between parts.
Inputs may be any that keep to these rules, and one draw needn't show every extreme that they name: `route_ids`: in the rows of one device no expert is named more than 128 times, a bound that some block reaches.
All inputs are finite; a program needn't handle non-finite values.
Results may differ from the reference program's by a relative error of at most 0.0006.
Values may be sent and summed in bfloat16 or wider, within the bound.
No kernel may reach another device: no remote copies, remote signals or barrier semaphores. Data moves between devices by JAX's collectives and lax.ppermute only.
A program may use at most 64 MiB of HBM per device.

```python
import math
import jax
import jax.numpy as jnp
import numpy as np
from jax import lax

D = 2048
FF = 384
TOPK = 4
PROJ = 128
QLEN = 32
PLEN = 64
TOK_DEV = 128
EXPERTS = 8
CAP = 128
NPASS = 32
TOKENS = 2048
NQ = 64
N_EXPERT = 4
N_QUERY = 2
N_DP = 2


def touch_ends(values, rng, smallest, top_value):
    shape = values.shape
    index_at = [jax.random.randint(jax.random.fold_in(rng, axis), (), 0, shape[axis]) for axis in range(len(shape))]
    values = values.at[tuple(index_at)].set(smallest)
    longest = shape.index(max(shape))
    index_at[longest] = (index_at[longest] + 1) % shape[longest]
    return values.at[tuple(index_at)].set(top_value)


def block_scale(stream_key, shape, cuts, least, high):
    factor_of = 1.0
    for axis_at, parts in cuts:
        heights = jax.random.uniform(jax.random.fold_in(jax.random.fold_in(stream_key, 6), axis_at), (parts,), jnp.float32, least / len(cuts), high / len(cuts))
        factor_of = factor_of * jnp.repeat(jnp.exp(heights), shape[axis_at] // parts).reshape((-1,) + (1,) * (len(shape) - 1 - axis_at))
    return factor_of


def shared_out(rng, own, number, rows, count, top, reach, skew):
    order = jax.random.permutation(rng, count)
    heavy_load, common = shares(count, rows * top, reach, skew, True), shares(count, rows * top, reach, skew, False)
    places = jnp.arange(count)

    def named(lengths, rotation):
        used = int((lengths > 0).sum())
        fixed = max(1, used // 4)
        moved = fixed + (places - fixed + rotation * (used - fixed)) % max(1, count - fixed)
        return jnp.zeros((count,), jnp.int32).at[order[jnp.where(places < fixed, places, moved)]].set(jnp.asarray(lengths, jnp.int32))

    lengths = jnp.where(number % 4 == 0, named(heavy_load, number // 4), named(common, number - number // 4 - 1))
    mixed = jax.random.permutation(jax.random.fold_in(own, 3), count)
    source_of, taker = mixed[0:count // 2 * 2:2], mixed[1:count // 2 * 2:2]
    slack = jnp.minimum(lengths[source_of] - 1, reach - lengths[taker]) // 2
    slack = jnp.where((source_of == order[0]) | (taker == order[0]) | (lengths[taker] == 0), 0, jnp.maximum(slack, 0))
    moved = jax.random.randint(jax.random.fold_in(own, 4), (count // 2,), 0, 1 << 20) % (slack + 1)
    lengths = lengths.at[source_of].add(-moved).at[taker].add(moved)
    members = jnp.searchsorted(jnp.cumsum(lengths), jnp.arange(rows * top), side="right").astype(jnp.int32)
    grid = members.reshape(top, rows).T
    grid = grid[jax.random.permutation(jax.random.fold_in(own, 1), rows)]
    rotation = jax.random.randint(jax.random.fold_in(own, 2), (rows, 1), 0, top)
    return jnp.take_along_axis(grid, (jnp.arange(top)[None, :] + rotation) % top, axis=1)


def shares(number_of, total, most, skew, full):
    loads = [(1 << 20) // math.isqrt(grade ** skew) + 1 for grade in range(1, number_of + 1)]
    largest = most if full else min(most, max(-(-total // number_of), total * loads[0] // sum(loads)))
    least = 1 if total - largest >= number_of - 1 else 0
    counts, spare = [largest] + [least] * (number_of - 1), total - largest - least * (number_of - 1)
    while spare > 0:
        movable = [i for i in range(1, number_of) if counts[i] < largest] or [i for i in range(1, number_of) if counts[i] < most]
        whole, budget = sum([loads[i] for i in movable]), spare
        for i in movable:
            addition = min(most - counts[i], max(1, budget * loads[i] // whole), spare)
            counts[i] = counts[i] + addition
            spare = spare - addition
    return np.array(counts)


def normal_values(rng, dims, spread, bound, split=(), kind=jnp.bfloat16):
    entries = jax.random.normal(rng, dims, jnp.float32) * spread
    if len(split) > 0:
        entries = block_scale(rng, dims, split, -0.22, 0.18) * entries
    return jnp.clip(entries, min=-bound, max=bound).astype(kind)


def setup_inputs(seed: int = 0, part: int = 0) -> dict:
    arg_keys = jax.random.split(jax.random.key(seed), 10)
    part_splits = jax.random.split(jax.random.fold_in(arg_keys[9], part), 10)
    tokens = normal_values(part_splits[0], (TOKENS, D), 1.0, 6.0, ((0, 16),))
    route_ids_keys = jax.random.split(jax.random.fold_in(part_splits[1], 1), TOKENS // TOK_DEV)
    route_ids_turns = jax.random.permutation(jax.random.fold_in(part_splits[1], 3), TOKENS // TOK_DEV)
    route_ids = jax.vmap(lambda own, number: shared_out(jax.random.fold_in(part_splits[1], 2), own, number, TOK_DEV, EXPERTS, TOPK, CAP, 2))(route_ids_keys, route_ids_turns).reshape((TOKENS, TOPK))
    gate_values = jnp.clip(jnp.exp(math.log(1.0) - 2.3025851 * jax.random.uniform(part_splits[2], (TOKENS, TOPK), jnp.float32) ** block_scale(part_splits[2], (TOKENS, TOPK), ((0, 16),), -0.2, 0.2)), 0.1, 1.0)
    passage_lengths = touch_ends(jax.random.randint(part_splits[3], (NPASS,), PLEN // 4, PLEN + 1), jax.random.fold_in(part_splits[3], 1), PLEN // 4, PLEN).astype(jnp.int32)
    gate_weight = normal_values(arg_keys[4], (EXPERTS, D, FF), D ** -0.5, 0.125, ((0, 8), (2, 2)))
    up_weight = normal_values(arg_keys[5], (EXPERTS, D, FF), D ** -0.5, 0.125, ((0, 8), (2, 2)))
    down_weight = normal_values(arg_keys[6], (EXPERTS, D, FF), FF ** -0.5, 0.3125, ((0, 8), (2, 2)))
    proj_weight = normal_values(arg_keys[7], (D, PROJ), D ** -0.5, 0.125)
    queries = normal_values(part_splits[8], (NQ, QLEN, PROJ), 0.1, 0.59765625, ((0, 2),))
    return dict(tokens=tokens, route_ids=route_ids, gate_values=gate_values, passage_lengths=passage_lengths, gate_weight=gate_weight, up_weight=up_weight, down_weight=down_weight, proj_weight=proj_weight, queries=queries)


def reference(tokens, route_ids, gate_values, passage_lengths, gate_weight, up_weight, down_weight, proj_weight, queries):
    token_count = tokens.shape[0]
    flat_routes = route_ids.reshape(-1)
    assignments = flat_routes.shape[0]
    flat_gates = gate_values.reshape(-1)
    room = N_EXPERT * N_QUERY * N_DP * CAP

    def per_expert(mixed_rows, expert_id):
        row_index = jnp.nonzero(flat_routes == expert_id, size=room, fill_value=assignments)[0]
        token_index = row_index // TOPK
        expert_rows = jnp.take(tokens, token_index, axis=0, mode='fill', fill_value=0)
        gate_act = jnp.dot(expert_rows, gate_weight[expert_id], preferred_element_type=jnp.float32)
        up_act = jnp.dot(expert_rows, up_weight[expert_id], preferred_element_type=jnp.float32)
        hidden = (jax.nn.silu(gate_act) * up_act).astype(jnp.bfloat16)
        expert_out = lax.dot_general(hidden, down_weight[expert_id], (((1,), (1,)), ((), ())), preferred_element_type=jnp.float32).astype(jnp.bfloat16)
        weights = jnp.take(flat_gates, row_index, mode='fill', fill_value=0)
        mixed_rows = mixed_rows.at[token_index].add(expert_out.astype(jnp.float32) * weights[:, None], mode='drop')
        return (mixed_rows, None)
    mixed_rows, _ = lax.scan(per_expert, tokens.astype(jnp.float32), jnp.arange(EXPERTS, dtype=jnp.int32))
    projected = jnp.dot(mixed_rows, proj_weight.astype(jnp.float32), precision=lax.Precision.HIGHEST)
    lengths_norm = jnp.sqrt(lax.optimization_barrier(jnp.sum(projected * projected, axis=-1, keepdims=True)) + 1e-06)
    embedding = (projected / lengths_norm).astype(jnp.bfloat16)
    passages = passage_lengths.shape[0]
    blocks = embedding.reshape(passages, PLEN, PROJ)
    live_mask = jnp.arange(PLEN, dtype=jnp.int32)[None, :] < passage_lengths[:, None]
    query_rows = queries.reshape(-1, PROJ)

    def score_passage(inputs):
        passage_block, passage_live = inputs
        raw_scores = jnp.dot(passage_block, query_rows.T, preferred_element_type=jnp.float32)
        raw_scores = jnp.where(passage_live[:, None], raw_scores, -jnp.inf)
        return lax.optimization_barrier(jnp.sum(lax.optimization_barrier(jnp.max(raw_scores, axis=0)).reshape(-1, QLEN), axis=-1))
    return lax.map(score_passage, (blocks, live_mask))
```

```python
import jax
import jax.numpy as jnp
from jax import lax
from jax.sharding import PartitionSpec as P

PLEN = 64
G, E, Q, D = "group", "expert", "query", "dp"


def matched(embedding, live_mask, block_queries):
    query_rows = block_queries.reshape(-1, block_queries.shape[-1])
    raw_scores = jnp.dot(embedding, query_rows.T, preferred_element_type=jnp.float32)
    raw_scores = jnp.where(live_mask[:, None], raw_scores, -jnp.inf)
    best_match = jnp.max(raw_scores.reshape(-1, PLEN, raw_scores.shape[-1]), axis=1)
    return jnp.sum(best_match.reshape(best_match.shape[0], -1, block_queries.shape[1]), axis=-1)


def embedded(projected):
    lengths_norm = jnp.sqrt(jnp.sum(projected * projected, axis=-1, keepdims=True) + 1e-06)
    return (projected / lengths_norm).astype(jnp.bfloat16)


def live_tokens(passage_lengths, tok_rows):
    position = jnp.arange(tok_rows, dtype=jnp.int32) % PLEN
    return position < jnp.repeat(passage_lengths, PLEN)


def by_dispatch(
    tokens, route_ids, gate_values, passage_lengths, gate_weight, up_weight, down_weight, proj_weight, queries
):
    tok_rows, model_width = tokens.shape
    top_count = route_ids.shape[1]
    experts = lax.axis_size(E) * lax.axis_size(Q)
    capacity = max(2, 2 * tok_rows * top_count // experts)
    assignments = tok_rows * top_count
    flat_routes = route_ids.reshape(-1)
    one_hot = flat_routes[:, None] == jnp.arange(experts, dtype=jnp.int32)[None, :]
    order = jnp.arange(assignments, dtype=jnp.int32)
    before = (order[None, :] < order[:, None]).astype(jnp.bfloat16)
    earlier = jnp.dot(before, one_hot.astype(jnp.bfloat16), preferred_element_type=jnp.float32)
    slot_index = jnp.sum(jnp.where(one_hot, earlier, 0.0), axis=1).astype(jnp.int32)
    slot_target = flat_routes * capacity + slot_index
    slot_owner = jnp.full((experts * capacity,), assignments, jnp.int32).at[slot_target].set(order)
    padded = jnp.concatenate([tokens, jnp.zeros((1, model_width), tokens.dtype)], axis=0)
    source_row = jnp.where(slot_owner < assignments, slot_owner // top_count, tok_rows)
    outgoing = padded[source_row].reshape(experts, capacity, model_width)
    arrived = lax.all_to_all(outgoing, (E, Q), split_axis=0, concat_axis=0, tiled=True)
    expert_rows = arrived.reshape(experts * capacity, model_width)
    gate_act = jnp.dot(
        expert_rows, lax.all_gather(gate_weight[0], D, axis=1, tiled=True), preferred_element_type=jnp.float32
    )
    up_act = jnp.dot(
        expert_rows, lax.all_gather(up_weight[0], D, axis=1, tiled=True), preferred_element_type=jnp.float32
    )
    hidden = (jax.nn.silu(gate_act) * up_act).astype(jnp.bfloat16)
    results = lax.dot_general(
        hidden,
        lax.all_gather(down_weight[0], D, axis=1, tiled=True),
        (((1,), (1,)), ((), ())),
        preferred_element_type=jnp.float32,
    ).astype(jnp.bfloat16)
    folded = jnp.dot(results, proj_weight, preferred_element_type=jnp.float32)
    returned_rows = lax.all_to_all(
        folded.reshape(experts, capacity, folded.shape[-1]), (E, Q), split_axis=0, concat_axis=0, tiled=True
    )
    picked = returned_rows.reshape(experts * capacity, folded.shape[-1])[slot_target]
    weights = gate_values.reshape(assignments, 1)
    projected = jnp.dot(tokens, proj_weight, preferred_element_type=jnp.float32) + jnp.sum(
        (picked * weights).reshape(tok_rows, top_count, folded.shape[-1]), axis=1
    )
    live_mask = live_tokens(passage_lengths, tok_rows)
    return matched(embedded(projected), live_mask, lax.all_gather(queries, Q, axis=0, tiled=True))


def hi_lo(values):
    high = values.astype(jnp.bfloat16)
    return high, (values - high.astype(jnp.float32)).astype(jnp.bfloat16)


def by_column(
    tokens, route_ids, gate_values, passage_lengths, gate_weight, up_weight, down_weight, proj_weight, queries
):
    tok_rows, model_width = tokens.shape
    hidden_part = gate_weight.shape[2]
    proj_width = proj_weight.shape[1]
    z, x, y, core = (lax.axis_index(a) for a in (E, Q, G, D))
    swap = [(0, 1), (1, 0)]
    ends, middle = [(1, 0), (2, 3)], [(1, 2), (2, 1)]

    near = lax.ppermute(tokens, E, [(i, i ^ 1) for i in range(4)])
    across = lax.ppermute(tokens, E, middle)
    far_inner = lax.ppermute(near, E, middle)
    end_two = lax.ppermute(across, E, ends)
    end_three = lax.ppermute(far_inner, E, ends)
    at_end = (z == 0) | (z == 3)

    folded = lax.dot_general(
        proj_weight, down_weight[0], (((0,), (0,)), ((), ())), preferred_element_type=jnp.float32
    )
    own = jnp.concatenate(
        [jnp.concatenate([gate_weight[0], up_weight[0]], axis=1), jnp.concatenate(hi_lo(folded), axis=1)], axis=0
    )
    half = own.shape[0] // 2
    mine = lax.dynamic_slice_in_dim(own, y * half, half, 0)
    half_x = lax.ppermute(mine, Q, swap)
    half_y = lax.ppermute(half_x, G, swap)
    own_pair = lax.ppermute(own, D, swap)
    pair_x = lax.ppermute(half_x, D, swap)
    pair_y = lax.ppermute(half_y, D, swap)

    def joined(here, there):
        return jnp.concatenate([jnp.where(y == 0, here, there), jnp.where(y == 0, there, here)], axis=0)

    other, other_pair = joined(half_x, half_y), joined(pair_x, pair_y)

    def through(rows, weights):
        act = jnp.dot(rows, weights[:model_width], preferred_element_type=jnp.float32)
        gate_act, up_act = act[:, :hidden_part], act[:, hidden_part:]
        hidden = (jax.nn.silu(gate_act) * up_act).astype(jnp.bfloat16)
        back = weights[model_width:]
        return sum(
            lax.dot_general(hidden, part, (((1,), (1,)), ((), ())), preferred_element_type=jnp.float32)
            for part in (back[:, :hidden_part], back[:, hidden_part:])
        )

    def results(rows):
        return jnp.concatenate(
            [through(rows, own) + through(rows, own_pair), through(rows, other) + through(rows, other_pair)], axis=1
        )

    blocks = [tokens, near, jnp.where(at_end, end_two, far_inner), jnp.where(at_end, end_three, across)]
    total = jnp.dot(tokens, proj_weight, preferred_element_type=jnp.float32)
    for k, rows in enumerate(blocks):
        got = results(rows)
        if k:
            got = lax.ppermute(got.astype(jnp.bfloat16), E, [(i, i ^ k) for i in range(4)]).astype(jnp.float32)
        for which in (0, 1):
            expert = (z ^ k) * 2 + (x ^ which)
            weight = jnp.sum(jnp.where(route_ids == expert, gate_values, 0.0), axis=1, keepdims=True)
            total = total + weight * got[:, which * proj_width : (which + 1) * proj_width]
    embedding = embedded(total)
    live_mask = live_tokens(passage_lengths, tok_rows)
    here = matched(embedding, live_mask, queries)
    there = matched(embedding, live_mask, lax.ppermute(queries, Q, swap))
    return jnp.where(x == 0, jnp.concatenate([here, there], axis=1), jnp.concatenate([there, here], axis=1))


def solution(mesh):
    in_specs = (
        P((G, E, Q, D), None),
        P((G, E, Q, D), None),
        P((G, E, Q, D), None),
        P((G, E, Q, D)),
        P((E, Q), None, D),
        P((E, Q), None, D),
        P((E, Q), None, D),
        P(),
        P((G, Q), None, None),
    )
    sizes = [mesh.shape[a] for a in (G, E, Q, D)]
    return jax.shard_map(
        by_column if sizes == [2, 4, 2, 2] else by_dispatch,
        mesh=mesh,
        in_specs=in_specs,
        out_specs=P((G, E, Q, D), None),
        check_vma=False,
    )
```

```python
import jax
import jax.numpy as jnp
from jax import lax
from jax.experimental import pallas as pl
from jax.experimental.pallas import tpu as pltpu
from jax.sharding import PartitionSpec as P

PLEN = 64
G, E, Q, D = "group", "expert", "query", "dp"


def matched(embedding, live_mask, block_queries):
    query_rows = block_queries.reshape(-1, block_queries.shape[-1])
    raw_scores = jnp.dot(embedding, query_rows.T, preferred_element_type=jnp.float32)
    raw_scores = jnp.where(live_mask[:, None], raw_scores, -jnp.inf)
    best_match = jnp.max(raw_scores.reshape(-1, PLEN, raw_scores.shape[-1]), axis=1)
    return jnp.sum(best_match.reshape(best_match.shape[0], -1, block_queries.shape[1]), axis=-1)


def embedded(projected):
    lengths_norm = jnp.sqrt(jnp.sum(projected * projected, axis=-1, keepdims=True) + 1e-06)
    return (projected / lengths_norm).astype(jnp.bfloat16)


def live_tokens(passage_lengths, tok_rows):
    position = jnp.arange(tok_rows, dtype=jnp.int32) % PLEN
    return position < jnp.repeat(passage_lengths, PLEN)


def by_dispatch(
    tokens, route_ids, gate_values, passage_lengths, gate_weight, up_weight, down_weight, proj_weight, queries
):
    tok_rows, model_width = tokens.shape
    top_count = route_ids.shape[1]
    experts = lax.axis_size(E) * lax.axis_size(Q)
    capacity = max(2, 2 * tok_rows * top_count // experts)
    assignments = tok_rows * top_count
    flat_routes = route_ids.reshape(-1)
    one_hot = flat_routes[:, None] == jnp.arange(experts, dtype=jnp.int32)[None, :]
    order = jnp.arange(assignments, dtype=jnp.int32)
    before = (order[None, :] < order[:, None]).astype(jnp.bfloat16)
    earlier = jnp.dot(before, one_hot.astype(jnp.bfloat16), preferred_element_type=jnp.float32)
    slot_index = jnp.sum(jnp.where(one_hot, earlier, 0.0), axis=1).astype(jnp.int32)
    slot_target = flat_routes * capacity + slot_index
    slot_owner = jnp.full((experts * capacity,), assignments, jnp.int32).at[slot_target].set(order)
    padded = jnp.concatenate([tokens, jnp.zeros((1, model_width), tokens.dtype)], axis=0)
    source_row = jnp.where(slot_owner < assignments, slot_owner // top_count, tok_rows)
    outgoing = padded[source_row].reshape(experts, capacity, model_width)
    arrived = lax.all_to_all(outgoing, (E, Q), split_axis=0, concat_axis=0, tiled=True)
    expert_rows = arrived.reshape(experts * capacity, model_width)
    gate_act = jnp.dot(
        expert_rows, lax.all_gather(gate_weight[0], D, axis=1, tiled=True), preferred_element_type=jnp.float32
    )
    up_act = jnp.dot(
        expert_rows, lax.all_gather(up_weight[0], D, axis=1, tiled=True), preferred_element_type=jnp.float32
    )
    hidden = (jax.nn.silu(gate_act) * up_act).astype(jnp.bfloat16)
    results = lax.dot_general(
        hidden,
        lax.all_gather(down_weight[0], D, axis=1, tiled=True),
        (((1,), (1,)), ((), ())),
        preferred_element_type=jnp.float32,
    ).astype(jnp.bfloat16)
    folded = jnp.dot(results, proj_weight, preferred_element_type=jnp.float32)
    returned_rows = lax.all_to_all(
        folded.reshape(experts, capacity, folded.shape[-1]), (E, Q), split_axis=0, concat_axis=0, tiled=True
    )
    picked = returned_rows.reshape(experts * capacity, folded.shape[-1])[slot_target]
    weights = gate_values.reshape(assignments, 1)
    projected = jnp.dot(tokens, proj_weight, preferred_element_type=jnp.float32) + jnp.sum(
        (picked * weights).reshape(tok_rows, top_count, folded.shape[-1]), axis=1
    )
    live_mask = live_tokens(passage_lengths, tok_rows)
    return matched(embedded(projected), live_mask, lax.all_gather(queries, Q, axis=0, tiled=True))


VMEM = pl.BlockSpec(memory_space=pltpu.VMEM)
SMEM = pl.BlockSpec(memory_space=pltpu.SMEM)
NT, TN = (((1,), (1,)), ((), ())), (((0,), (0,)), ((), ()))


def dot(a, b, dims=(((1,), (0,)), ((), ()))):
    return lax.dot_general(a, b, dims, preferred_element_type=jnp.float32)


def kernel(body, operands, outs, flops, smem=()):
    moved = sum(a.size * a.dtype.itemsize for a in operands)
    return pl.pallas_call(
        body,
        out_shape=[jax.ShapeDtypeStruct(shape, dtype) for shape, dtype in outs],
        in_specs=[SMEM if i in smem else VMEM for i in range(len(operands))],
        out_specs=[VMEM] * len(outs),
        compiler_params=pltpu.CompilerParams(vmem_limit_bytes=24 * 2**20),
        cost_estimate=pl.CostEstimate(flops=int(flops), bytes_accessed=int(moved), transcendentals=0),
    )(*operands)


FOLD = 16


def pack_body(tokens, gate, up, down, proj, pack, half, base):
    rows = gate.shape[0]
    width = proj.shape[1]
    pack[:rows, :] = gate[...]
    pack[rows : 2 * rows, :] = up[...]
    folded = dot(down[...], proj[...])
    high = folded.astype(jnp.bfloat16)
    low = (folded - high.astype(jnp.float32)).astype(jnp.bfloat16)
    pack[2 * rows :, :] = jnp.zeros((2 * FOLD, pack.shape[1]), jnp.bfloat16)
    for i in range(rows // FOLD):
        pack[2 * rows : 2 * rows + FOLD, i * width : (i + 1) * width] = high[i * FOLD : (i + 1) * FOLD]
        pack[2 * rows + FOLD :, i * width : (i + 1) * width] = low[i * FOLD : (i + 1) * FOLD]
    part = half.shape[0]
    for y in range(2):

        @pl.when(lax.axis_index(G) == y)
        def _():
            half[...] = pack[y * part : (y + 1) * part, :]

    base[...] = dot(tokens[...], proj[...]).T


def folded_parts(tile, rows, width):
    return [
        jnp.concatenate([tile[k * FOLD : (k + 1) * FOLD, i * width : (i + 1) * width] for i in range(rows // FOLD)], axis=0)
        for k in range(2)
    ]


def finish(act, tile, width):
    rows = act.shape[0] // 2
    gate_act, up_act = act[:rows], act[rows:]
    hidden = (gate_act / (1.0 + jnp.exp(-gate_act)) * up_act).astype(jnp.bfloat16)
    return sum(dot(part, hidden, TN) for part in folded_parts(tile, rows, width))


def through_whole(x, packs, width):
    total = None
    for pack in packs:
        rows = pack.shape[0] - 2 * FOLD
        part = finish(dot(pack[:rows, :], x, NT), pack[rows:, :], width)
        total = part if total is None else total + part
    return total


def through_halves(x, halves, width):
    first = lax.axis_index(G) == 0
    total = None
    for mine, others in halves:
        a, b = dot(mine[...], x, NT), dot(others[...], x, NT)
        rows = mine.shape[0]
        act = jnp.concatenate([jnp.where(first, a, b), jnp.where(first, b, a)[: rows - 2 * FOLD]], axis=0)
        tile = jnp.where(first, others[rows - 2 * FOLD :, :], mine[rows - 2 * FOLD :, :])
        part = finish(act, tile, width)
        total = part if total is None else total + part
    return total


def at_end():
    z = lax.axis_index(E)
    return (z == 0) | (z == lax.axis_size(E) - 1)


def first_body(tokens, near, own, pair, here, back):
    width = here.shape[0]
    x = jnp.concatenate([tokens[...], near[...]], axis=0)
    got = through_whole(x, (own, pair), width)
    here[...] = got[:, : tokens.shape[0]]
    back[...] = got[:, tokens.shape[0] :].astype(back.dtype)


def second_body(tokens, near, end_two, far_inner, own, pair, ox, oy, px, py, here, back_near, back_two):
    width = here.shape[0]
    n = tokens.shape[0]
    two = jnp.where(at_end(), end_two[...], far_inner[...])
    back_two[:width, :] = through_whole(two, (own, pair), width).astype(back_two.dtype)
    x = jnp.concatenate([tokens[...], near[...], two], axis=0)
    got = through_halves(x, ((ox, oy), (px, py)), width)
    here[...] = got[:, :n]
    back_near[...] = got[:, n : 2 * n].astype(back_near.dtype)
    back_two[width:, :] = got[:, 2 * n :].astype(back_two.dtype)


def third_body(end_three, across, own, pair, ox, oy, px, py, back_three):
    width = back_three.shape[0] // 2
    three = jnp.where(at_end(), end_three[...], across[...])
    back_three[:width, :] = through_whole(three, (own, pair), width).astype(back_three.dtype)
    back_three[width:, :] = through_halves(three, ((ox, oy), (px, py)), width).astype(back_three.dtype)


def score_body(lengths, base, here, here_other, near, near_other, two, three, routes, gates, queries, others, scores):
    z, x = lax.axis_index(E), lax.axis_index(Q)
    width, tokens = base.shape
    total = base[...]
    route, gate = routes[...], gates[...]
    sent = [
        (here[...], here_other[...]),
        (near[...], near_other[...]),
        (two[:width, :], two[width:, :]),
        (three[:width, :], three[width:, :]),
    ]
    for k, pair in enumerate(sent):
        for which in (0, 1):
            expert = (z ^ k) * 2 + (x ^ which)
            weight = jnp.sum(jnp.where(route == expert, gate, 0.0), axis=0, keepdims=True)
            total = total + weight * pair[which].astype(jnp.float32)
    norm = jnp.sqrt(jnp.sum(total * total, axis=0, keepdims=True) + 1e-06)
    embedding = (total / norm).T.astype(jnp.bfloat16)
    count, span = queries.shape[0], queries.shape[0] * 2 // scores.shape[1]
    query_at = lax.broadcasted_iota(jnp.int32, (count, scores.shape[1]), 0) // span
    column = lax.broadcasted_iota(jnp.int32, (count, scores.shape[1]), 1)
    result = jnp.zeros(scores.shape, jnp.float32)
    for which, block in ((0, queries), (1, others)):
        raw = dot(embedding, block[...], NT)
        best = []
        for p in range(tokens // PLEN):
            live = lax.broadcasted_iota(jnp.int32, (PLEN, count), 0) < lengths[p]
            best.append(
                jnp.max(jnp.where(live, raw[p * PLEN : (p + 1) * PLEN], -jnp.inf), axis=0, keepdims=True)
            )
        chosen = (column == query_at + (x ^ which) * (count // span)).astype(jnp.float32)
        result = result + lax.dot_general(
            jnp.concatenate(best, axis=0), chosen, (((1,), (0,)), ((), ())),
            precision=lax.Precision.HIGHEST, preferred_element_type=jnp.float32,
        )
    scores[...] = result


def by_column(
    tokens, route_ids, gate_values, passage_lengths, gate_weight, up_weight, down_weight, proj_weight, queries
):
    n, model_width = tokens.shape
    hidden_part = gate_weight.shape[2]
    width = proj_weight.shape[1]
    swap = [(0, 1), (1, 0)]
    ends, middle = [(1, 0), (2, 3)], [(1, 2), (2, 1)]
    f32, bf16 = jnp.float32, jnp.bfloat16

    near = lax.ppermute(tokens, E, [(i, i ^ 1) for i in range(4)])
    across = lax.ppermute(tokens, E, middle)
    far_inner = lax.ppermute(near, E, middle)
    end_two = lax.ppermute(across, E, ends)
    end_three = lax.ppermute(far_inner, E, ends)

    pack_rows = 2 * hidden_part + 2 * FOLD
    own, half, base = kernel(
        pack_body,
        [tokens, gate_weight[0].T, up_weight[0].T, down_weight[0].T, proj_weight],
        [((pack_rows, model_width), bf16), ((pack_rows // 2, model_width), bf16), ((width, n), f32)],
        2 * (hidden_part + n) * model_width * width,
    )
    pair = lax.ppermute(own, D, swap)
    half_x = lax.ppermute(half, Q, swap)
    half_y = lax.ppermute(half_x, G, swap)
    pair_x = lax.ppermute(half_x, D, swap)
    pair_y = lax.ppermute(half_y, D, swap)
    other_queries = lax.ppermute(queries, Q, swap)

    work = 2 * n * model_width * 4 * hidden_part
    here, back_near = kernel(
        first_body, [tokens, near, own, pair], [((width, n), f32), ((width, n), bf16)], 2 * work
    )
    other = [half_x, half_y, pair_x, pair_y]
    here_other, back_near_other, back_two = kernel(
        second_body,
        [tokens, near, end_two, far_inner, own, pair, *other],
        [((width, n), f32), ((width, n), bf16), ((2 * width, n), bf16)],
        4 * work,
    )
    (back_three,) = kernel(
        third_body, [end_three, across, own, pair, *other], [((2 * width, n), bf16)], 2 * work
    )
    from_near, from_near_other, two, three = (
        lax.ppermute(a, E, [(i, i ^ k) for i in range(4)])
        for a, k in ((back_near, 1), (back_near_other, 1), (back_two, 2), (back_three, 3))
    )
    rows = queries.shape[0] * queries.shape[1]
    (scores,) = kernel(
        score_body,
        [
            passage_lengths, base, here, here_other, from_near, from_near_other, two, three,
            route_ids.T, gate_values.T, queries.reshape(rows, width), other_queries.reshape(rows, width),
        ],
        [((n // PLEN, 2 * queries.shape[0]), f32)],
        4 * n * width * rows,
        smem=(0,),
    )
    return scores


def solution(mesh):
    in_specs = (
        P((G, E, Q, D), None),
        P((G, E, Q, D), None),
        P((G, E, Q, D), None),
        P((G, E, Q, D)),
        P((E, Q), None, D),
        P((E, Q), None, D),
        P((E, Q), None, D),
        P(),
        P((G, Q), None, None),
    )
    sizes = [mesh.shape[a] for a in (G, E, Q, D)]
    return jax.shard_map(
        by_column if sizes == [2, 4, 2, 2] else by_dispatch,
        mesh=mesh,
        in_specs=in_specs,
        out_specs=P((G, E, Q, D), None),
        check_vma=False,
    )
```

```python
import jax
import jax.numpy as jnp
from jax import lax
from jax.experimental import pallas as pl
from jax.experimental.pallas import tpu as pltpu
from jax.sharding import PartitionSpec as P

PLEN = 64
G, E, Q, D = "group", "expert", "query", "dp"


def matched(embedding, live_mask, block_queries):
    query_rows = block_queries.reshape(-1, block_queries.shape[-1])
    raw_scores = jnp.dot(embedding, query_rows.T, preferred_element_type=jnp.float32)
    raw_scores = jnp.where(live_mask[:, None], raw_scores, -jnp.inf)
    best_match = jnp.max(raw_scores.reshape(-1, PLEN, raw_scores.shape[-1]), axis=1)
    return jnp.sum(best_match.reshape(best_match.shape[0], -1, block_queries.shape[1]), axis=-1)


def embedded(projected):
    lengths_norm = jnp.sqrt(jnp.sum(projected * projected, axis=-1, keepdims=True) + 1e-06)
    return (projected / lengths_norm).astype(jnp.bfloat16)


def live_tokens(passage_lengths, tok_rows):
    position = jnp.arange(tok_rows, dtype=jnp.int32) % PLEN
    return position < jnp.repeat(passage_lengths, PLEN)


def by_dispatch(
    tokens, route_ids, gate_values, passage_lengths, gate_weight, up_weight, down_weight, proj_weight, queries
):
    tok_rows, model_width = tokens.shape
    top_count = route_ids.shape[1]
    experts = lax.axis_size(E) * lax.axis_size(Q)
    capacity = max(2, 2 * tok_rows * top_count // experts)
    assignments = tok_rows * top_count
    flat_routes = route_ids.reshape(-1)
    one_hot = flat_routes[:, None] == jnp.arange(experts, dtype=jnp.int32)[None, :]
    order = jnp.arange(assignments, dtype=jnp.int32)
    before = (order[None, :] < order[:, None]).astype(jnp.bfloat16)
    earlier = jnp.dot(before, one_hot.astype(jnp.bfloat16), preferred_element_type=jnp.float32)
    slot_index = jnp.sum(jnp.where(one_hot, earlier, 0.0), axis=1).astype(jnp.int32)
    slot_target = flat_routes * capacity + slot_index
    slot_owner = jnp.full((experts * capacity,), assignments, jnp.int32).at[slot_target].set(order)
    padded = jnp.concatenate([tokens, jnp.zeros((1, model_width), tokens.dtype)], axis=0)
    source_row = jnp.where(slot_owner < assignments, slot_owner // top_count, tok_rows)
    outgoing = padded[source_row].reshape(experts, capacity, model_width)
    arrived = lax.all_to_all(outgoing, (E, Q), split_axis=0, concat_axis=0, tiled=True)
    expert_rows = arrived.reshape(experts * capacity, model_width)
    gate_act = jnp.dot(
        expert_rows, lax.all_gather(gate_weight[0], D, axis=1, tiled=True), preferred_element_type=jnp.float32
    )
    up_act = jnp.dot(
        expert_rows, lax.all_gather(up_weight[0], D, axis=1, tiled=True), preferred_element_type=jnp.float32
    )
    hidden = (jax.nn.silu(gate_act) * up_act).astype(jnp.bfloat16)
    results = lax.dot_general(
        hidden,
        lax.all_gather(down_weight[0], D, axis=1, tiled=True),
        (((1,), (1,)), ((), ())),
        preferred_element_type=jnp.float32,
    ).astype(jnp.bfloat16)
    folded = jnp.dot(results, proj_weight, preferred_element_type=jnp.float32)
    returned_rows = lax.all_to_all(
        folded.reshape(experts, capacity, folded.shape[-1]), (E, Q), split_axis=0, concat_axis=0, tiled=True
    )
    picked = returned_rows.reshape(experts * capacity, folded.shape[-1])[slot_target]
    weights = gate_values.reshape(assignments, 1)
    projected = jnp.dot(tokens, proj_weight, preferred_element_type=jnp.float32) + jnp.sum(
        (picked * weights).reshape(tok_rows, top_count, folded.shape[-1]), axis=1
    )
    live_mask = live_tokens(passage_lengths, tok_rows)
    return matched(embedded(projected), live_mask, lax.all_gather(queries, Q, axis=0, tiled=True))


VMEM = pl.BlockSpec(memory_space=pltpu.VMEM)
SMEM = pl.BlockSpec(memory_space=pltpu.SMEM)
NT, TN = (((1,), (1,)), ((), ())), (((0,), (0,)), ((), ()))


def dot(a, b, dims=(((1,), (0,)), ((), ()))):
    return lax.dot_general(a, b, dims, preferred_element_type=jnp.float32)


def whole_block(a):
    return pl.BlockSpec(a.shape, lambda *_: (0,) * a.ndim)


def tied(values, after):
    def body(*refs):
        for i in range(len(values)):
            refs[len(values) + len(after) + i][...] = refs[i][...]

    return pl.pallas_call(
        body,
        out_shape=[jax.ShapeDtypeStruct(a.shape, a.dtype) for a in values],
        in_specs=[VMEM] * len(values) + [pl.BlockSpec(memory_space=pl.ANY)] * len(after),
        out_specs=[VMEM] * len(values),
        compiler_params=pltpu.CompilerParams(vmem_limit_bytes=8 * 2**20),
    )(*values, *after)


def kernel(body, operands, outs, flops, smem=(), fetched=(), limit=24):
    moved = sum(a.size * a.dtype.itemsize for a in operands)
    return pl.pallas_call(
        body,
        out_shape=[jax.ShapeDtypeStruct(shape, dtype) for shape, dtype in outs],
        in_specs=[
            SMEM if i in smem else whole_block(a) if i in fetched else VMEM for i, a in enumerate(operands)
        ],
        out_specs=[VMEM] * len(outs),
        compiler_params=pltpu.CompilerParams(vmem_limit_bytes=limit * 2**20),
        cost_estimate=pl.CostEstimate(flops=int(flops), bytes_accessed=int(moved), transcendentals=0),
    )(*operands)


FOLD = 16


def pack_body(tokens, gate, up, down, proj, pack, part, rest, base):
    rows = gate.shape[0]
    width = proj.shape[1]
    pack[:rows, :] = gate[...]
    pack[rows : 2 * rows, :] = up[...]
    folded = dot(down[...], proj[...]).astype(jnp.bfloat16)
    pack[2 * rows :, :] = jnp.zeros((FOLD, pack.shape[1]), jnp.bfloat16)
    for i in range(rows // FOLD):
        pack[2 * rows :, i * width : (i + 1) * width] = folded[i * FOLD : (i + 1) * FOLD]
    size = part.shape[0]
    for y in range(2):

        @pl.when(lax.axis_index(G) == y)
        def _():
            part[...] = pack[y * size : (y + 1) * size, :]

    rest[...] = pack[2 * size :, :]
    base[...] = dot(tokens[...], proj[...]).T


def finish(act, tile, width):
    rows = act.shape[0] // 2
    gate_act, up_act = act[:rows], act[rows:]
    hidden = (gate_act / (1.0 + jnp.exp(-gate_act)) * up_act).astype(jnp.bfloat16)
    folded = jnp.concatenate([tile[:, i * width : (i + 1) * width] for i in range(rows // FOLD)], axis=0)
    return dot(folded, hidden, TN)


def through_whole(x, packs, width):
    total = None
    for pack in packs:
        rows = pack.shape[0] - FOLD
        part = finish(dot(pack[:rows, :], x, NT), pack[rows:, :], width)
        total = part if total is None else total + part
    return total


def through_parts(x, packs, width):
    first = lax.axis_index(G) == 0
    total = None
    for mine, others, rest in packs:
        a, b = dot(mine[...], x, NT), dot(others[...], x, NT)
        rows = rest.shape[0] - FOLD
        act = [jnp.where(first, a, b), jnp.where(first, b, a), dot(rest[:rows, :], x, NT)]
        part = finish(jnp.concatenate(act, axis=0), rest[rows:, :], width)
        total = part if total is None else total + part
    return total


def at_end():
    z = lax.axis_index(E)
    return (z == 0) | (z == lax.axis_size(E) - 1)


def first_body(tokens, near, own, pair, got):
    x = jnp.concatenate([tokens[...], near[...]], axis=0)
    got[...] = through_whole(x, (own, pair), got.shape[0])


def second_body(tokens, near, end_two, far_inner, own, pair, ox, oy, oz, px, py, pz, got_own, here, back_near, back_two):
    n, width = tokens.shape[0], got_own.shape[0]
    two = jnp.where(at_end(), end_two[...], far_inner[...])
    back_two[:width, :] = through_whole(two, (own, pair), width).astype(back_two.dtype)
    x = jnp.concatenate([tokens[...], near[...], two], axis=0)
    got = through_parts(x, ((ox, oy, oz), (px, py, pz)), width)
    here[:width, :] = got_own[:, :n]
    here[width:, :] = got[:, :n]
    back_near[:width, :] = got_own[:, n:].astype(back_near.dtype)
    back_near[width:, :] = got[:, n : 2 * n].astype(back_near.dtype)
    back_two[width:, :] = got[:, 2 * n :].astype(back_two.dtype)


def third_body(end_three, across, own, pair, ox, oy, oz, px, py, pz, back_three):
    width = back_three.shape[0] // 2
    three = jnp.where(at_end(), end_three[...], across[...])
    back_three[:width, :] = through_whole(three, (own, pair), width).astype(back_three.dtype)
    back_three[width:, :] = through_parts(three, ((ox, oy, oz), (px, py, pz)), width).astype(back_three.dtype)


def score_body(lengths, base, here, near, two, three, routes, gates, queries, others, scores):
    z, x = lax.axis_index(E), lax.axis_index(Q)
    width, tokens = base.shape
    total = base[...]
    route, gate = routes[...], gates[...]
    for k, sent in enumerate((here, near, two, three)):
        for which in (0, 1):
            expert = (z ^ k) * 2 + (x ^ which)
            weight = jnp.sum(jnp.where(route == expert, gate, 0.0), axis=0, keepdims=True)
            total = total + weight * sent[which * width : (which + 1) * width, :].astype(jnp.float32)
    norm = jnp.sqrt(jnp.sum(total * total, axis=0, keepdims=True) + 1e-06)
    embedding = (total / norm).T.astype(jnp.bfloat16)
    count, span = queries.shape[0], queries.shape[0] * 2 // scores.shape[1]
    query_at = lax.broadcasted_iota(jnp.int32, (count, scores.shape[1]), 0) // span
    column = lax.broadcasted_iota(jnp.int32, (count, scores.shape[1]), 1)
    result = jnp.zeros(scores.shape, jnp.float32)
    for which, block in ((0, queries), (1, others)):
        raw = dot(embedding, block[...], NT)
        best = []
        for p in range(tokens // PLEN):
            live = lax.broadcasted_iota(jnp.int32, (PLEN, count), 0) < lengths[p]
            best.append(
                jnp.max(jnp.where(live, raw[p * PLEN : (p + 1) * PLEN], -jnp.inf), axis=0, keepdims=True)
            )
        chosen = (column == query_at + (x ^ which) * (count // span)).astype(jnp.float32)
        result = result + lax.dot_general(
            jnp.concatenate(best, axis=0), chosen, (((1,), (0,)), ((), ())),
            precision=lax.Precision.HIGHEST, preferred_element_type=jnp.float32,
        )
    scores[...] = result


def by_column(
    tokens, route_ids, gate_values, passage_lengths, gate_weight, up_weight, down_weight, proj_weight, queries
):
    n, model_width = tokens.shape
    hidden_part = gate_weight.shape[2]
    width = proj_weight.shape[1]
    swap = [(0, 1), (1, 0)]
    ends, middle = [(1, 0), (2, 3)], [(1, 2), (2, 1)]
    f32, bf16 = jnp.float32, jnp.bfloat16

    pack_rows = 2 * hidden_part + FOLD
    part_rows = pack_rows // 3 // 16 * 16
    own, part, rest, base = kernel(
        pack_body,
        [tokens, gate_weight[0].T, up_weight[0].T, down_weight[0].T, proj_weight],
        [((r, model_width), bf16) for r in (pack_rows, part_rows, pack_rows - 2 * part_rows)] + [((width, n), f32)],
        2 * (hidden_part + n) * model_width * width,
        fetched=(0, 1, 2, 3, 4),
        limit=56,
    )
    near = lax.ppermute(tokens, E, [(i, i ^ 1) for i in range(4)])
    across = lax.ppermute(tokens, E, middle)
    part_x = lax.ppermute(part, Q, swap)
    pair = lax.ppermute(own, D, swap)
    part_x, rest = tied([part_x, rest], [near, across])

    far_inner = lax.ppermute(near, E, middle)
    end_two = lax.ppermute(across, E, ends)
    rest_x = lax.ppermute(rest, Q, swap)
    part_y = lax.ppermute(part_x, G, swap)
    pair_part_x = lax.ppermute(part_x, D, swap)
    work = 2 * n * model_width * 4 * hidden_part
    (got_own,) = kernel(first_body, [tokens, near, own, pair], [((width, 2 * n), f32)], 2 * work, fetched=(0,))

    end_three = lax.ppermute(far_inner, E, ends)
    rest_x, part_y = tied([rest_x, part_y], [far_inner, end_two, got_own])
    pair_rest_x = lax.ppermute(rest_x, D, swap)
    pair_part_y = lax.ppermute(part_y, D, swap)
    other_queries = lax.ppermute(queries, Q, swap)

    other = [part_x, part_y, rest_x, pair_part_x, pair_part_y, pair_rest_x]
    both = (2 * width, n)
    here, back_near, back_two = kernel(
        second_body,
        [tokens, near, end_two, far_inner, own, pair, *other, got_own],
        [(both, f32), (both, bf16), (both, bf16)],
        4 * work,
        fetched=(0,),
    )
    (back_three,) = kernel(third_body, [end_three, across, own, pair, *other], [(both, bf16)], 2 * work)
    from_near, two, three = (
        lax.ppermute(a, E, [(i, i ^ k) for i in range(4)])
        for k, a in ((1, back_near), (2, back_two), (3, back_three))
    )
    rows = queries.shape[0] * queries.shape[1]
    (scores,) = kernel(
        score_body,
        [
            passage_lengths, base, here, from_near, two, three, route_ids.T, gate_values.T,
            queries.reshape(rows, width), other_queries.reshape(rows, width),
        ],
        [((n // PLEN, 2 * queries.shape[0]), f32)],
        4 * n * width * rows,
        smem=(0,),
    )
    return scores


def solution(mesh):
    in_specs = (
        P((G, E, Q, D), None),
        P((G, E, Q, D), None),
        P((G, E, Q, D), None),
        P((G, E, Q, D)),
        P((E, Q), None, D),
        P((E, Q), None, D),
        P((E, Q), None, D),
        P(),
        P((G, Q), None, None),
    )
    sizes = [mesh.shape[a] for a in (G, E, Q, D)]
    return jax.shard_map(
        by_column if sizes == [2, 4, 2, 2] else by_dispatch,
        mesh=mesh,
        in_specs=in_specs,
        out_specs=P((G, E, Q, D), None),
        check_vma=False,
    )
```

```python
import jax
import jax.numpy as jnp
from jax import lax
from jax.experimental import pallas as pl
from jax.experimental.pallas import tpu as pltpu
from jax.sharding import PartitionSpec as P

PLEN = 64
G, E, Q, D = "group", "expert", "query", "dp"


def matched(embedding, live_mask, block_queries):
    query_rows = block_queries.reshape(-1, block_queries.shape[-1])
    raw_scores = jnp.dot(embedding, query_rows.T, preferred_element_type=jnp.float32)
    raw_scores = jnp.where(live_mask[:, None], raw_scores, -jnp.inf)
    best_match = jnp.max(raw_scores.reshape(-1, PLEN, raw_scores.shape[-1]), axis=1)
    return jnp.sum(best_match.reshape(best_match.shape[0], -1, block_queries.shape[1]), axis=-1)


def embedded(projected):
    lengths_norm = jnp.sqrt(jnp.sum(projected * projected, axis=-1, keepdims=True) + 1e-06)
    return (projected / lengths_norm).astype(jnp.bfloat16)


def live_tokens(passage_lengths, tok_rows):
    position = jnp.arange(tok_rows, dtype=jnp.int32) % PLEN
    return position < jnp.repeat(passage_lengths, PLEN)


def by_dispatch(
    tokens, route_ids, gate_values, passage_lengths, gate_weight, up_weight, down_weight, proj_weight, queries
):
    tok_rows, model_width = tokens.shape
    top_count = route_ids.shape[1]
    experts = lax.axis_size(E) * lax.axis_size(Q)
    capacity = max(2, 2 * tok_rows * top_count // experts)
    assignments = tok_rows * top_count
    flat_routes = route_ids.reshape(-1)
    one_hot = flat_routes[:, None] == jnp.arange(experts, dtype=jnp.int32)[None, :]
    order = jnp.arange(assignments, dtype=jnp.int32)
    before = (order[None, :] < order[:, None]).astype(jnp.bfloat16)
    earlier = jnp.dot(before, one_hot.astype(jnp.bfloat16), preferred_element_type=jnp.float32)
    slot_index = jnp.sum(jnp.where(one_hot, earlier, 0.0), axis=1).astype(jnp.int32)
    slot_target = flat_routes * capacity + slot_index
    slot_owner = jnp.full((experts * capacity,), assignments, jnp.int32).at[slot_target].set(order)
    padded = jnp.concatenate([tokens, jnp.zeros((1, model_width), tokens.dtype)], axis=0)
    source_row = jnp.where(slot_owner < assignments, slot_owner // top_count, tok_rows)
    outgoing = padded[source_row].reshape(experts, capacity, model_width)
    arrived = lax.all_to_all(outgoing, (E, Q), split_axis=0, concat_axis=0, tiled=True)
    expert_rows = arrived.reshape(experts * capacity, model_width)
    gate_act = jnp.dot(
        expert_rows, lax.all_gather(gate_weight[0], D, axis=1, tiled=True), preferred_element_type=jnp.float32
    )
    up_act = jnp.dot(
        expert_rows, lax.all_gather(up_weight[0], D, axis=1, tiled=True), preferred_element_type=jnp.float32
    )
    hidden = (jax.nn.silu(gate_act) * up_act).astype(jnp.bfloat16)
    results = lax.dot_general(
        hidden,
        lax.all_gather(down_weight[0], D, axis=1, tiled=True),
        (((1,), (1,)), ((), ())),
        preferred_element_type=jnp.float32,
    ).astype(jnp.bfloat16)
    folded = jnp.dot(results, proj_weight, preferred_element_type=jnp.float32)
    returned_rows = lax.all_to_all(
        folded.reshape(experts, capacity, folded.shape[-1]), (E, Q), split_axis=0, concat_axis=0, tiled=True
    )
    picked = returned_rows.reshape(experts * capacity, folded.shape[-1])[slot_target]
    weights = gate_values.reshape(assignments, 1)
    projected = jnp.dot(tokens, proj_weight, preferred_element_type=jnp.float32) + jnp.sum(
        (picked * weights).reshape(tok_rows, top_count, folded.shape[-1]), axis=1
    )
    live_mask = live_tokens(passage_lengths, tok_rows)
    return matched(embedded(projected), live_mask, lax.all_gather(queries, Q, axis=0, tiled=True))


VMEM = pl.BlockSpec(memory_space=pltpu.VMEM)
SMEM = pl.BlockSpec(memory_space=pltpu.SMEM)
NT, TN = (((1,), (1,)), ((), ())), (((0,), (0,)), ((), ()))


def dot(a, b, dims=(((1,), (0,)), ((), ()))):
    return lax.dot_general(a, b, dims, preferred_element_type=jnp.float32)


def whole_block(a):
    return pl.BlockSpec(a.shape, lambda *_: (0,) * a.ndim)


def tied(values, after, parts):
    def body(*refs):
        outs = refs[len(values) + len(after) :]
        for i in range(len(values)):
            rows = outs[parts * i].shape[0]
            for p in range(parts):
                outs[parts * i + p][...] = refs[i][p * rows : (p + 1) * rows, :]

    blocks = [jax.ShapeDtypeStruct((a.shape[0] // parts, a.shape[1]), a.dtype) for a in values for _ in range(parts)]

    return pl.pallas_call(
        body,
        out_shape=blocks,
        in_specs=[VMEM] * len(values) + [pl.BlockSpec(memory_space=pl.ANY)] * len(after),
        out_specs=[VMEM] * len(blocks),
        compiler_params=pltpu.CompilerParams(vmem_limit_bytes=8 * 2**20),
    )(*values, *after)


def kernel(body, operands, outs, smem=(), fetched=(), limit=24, flops=0):
    return pl.pallas_call(
        body,
        out_shape=[jax.ShapeDtypeStruct(shape, dtype) for shape, dtype in outs],
        in_specs=[
            SMEM if i in smem else whole_block(a) if i in fetched else VMEM for i, a in enumerate(operands)
        ],
        out_specs=[VMEM] * len(outs),
        compiler_params=pltpu.CompilerParams(vmem_limit_bytes=limit * 2**20),
        cost_estimate=pl.CostEstimate(flops=flops, bytes_accessed=0, transcendentals=0),
    )(*operands)


FOLD = 16


def part_body(gate, up, part):
    rows = part.shape[0]
    part[...] = jnp.where(lax.axis_index(G) == 0, gate[:rows, :], up[:rows, :])


def fold_body(
    lengths, tokens, gate, up, down, proj, routes, gates,
    fold, rest_gate, rest_up, base, weights, live, chosen,
):
    rows, width = down.shape[0], proj.shape[1]
    folded = dot(down[...], proj[...]).astype(jnp.bfloat16)
    fold[...] = jnp.zeros_like(fold)
    for i in range(rows // FOLD):
        fold[:, i * width : (i + 1) * width] = folded[i * FOLD : (i + 1) * FOLD]
    left = rest_up.shape[0]
    rest_gate[:left, :] = gate[rows - left :, :]
    rest_gate[left:, :] = fold[...]
    rest_up[...] = up[rows - left :, :]
    base[...] = dot(tokens[...], proj[...]).T
    z, x = lax.axis_index(E), lax.axis_index(Q)
    for i in range(weights.shape[0]):
        expert = (z ^ (i // 2)) * 2 + (x ^ (i % 2))
        weights[i : i + 1, :] = jnp.sum(jnp.where(routes[...] == expert, gates[...], 0.0), axis=0, keepdims=True)
    position = lax.broadcasted_iota(jnp.int32, (PLEN, live.shape[1]), 0)
    for p in range(live.shape[0] // PLEN):
        live[p * PLEN : (p + 1) * PLEN, :] = jnp.where(position < lengths[p], 0.0, -jnp.inf)
    count, span = chosen.shape[0] // 2, chosen.shape[0] // chosen.shape[1]
    query = lax.broadcasted_iota(jnp.int32, (count, chosen.shape[1]), 0) // span
    column = lax.broadcasted_iota(jnp.int32, (count, chosen.shape[1]), 1)
    for w in (0, 1):
        hit = jnp.where(column == query + (x ^ w) * (count // span), 1.0, 0.0)
        chosen[w * count : (w + 1) * count, :] = hit.astype(chosen.dtype)


def finish(act, tile, width):
    rows = act.shape[0] // 2
    gate_act, up_act = act[:rows], act[rows:]
    hidden = (gate_act / (1.0 + jnp.exp(-gate_act)) * up_act).astype(jnp.bfloat16)
    folded = jnp.concatenate([tile[:, i * width : (i + 1) * width] for i in range(rows // FOLD)], axis=0)
    return dot(folded, hidden, TN)


def through(x, cores, width):
    total = None
    for blocks, fold in cores:
        part = finish(dot(jnp.concatenate(blocks, axis=0), x, NT), fold, width)
        total = part if total is None else total + part
    return total


def own_cores(gate, up, fold, pair_gate, pair_up, pair_fold):
    return [([gate[...], up[...]], fold[...]), ([pair_gate[...], pair_up[...]], pair_fold[...])]


def other_cores(*refs):
    first = lax.axis_index(G) == 0
    cores = []
    for mine, others, rest_gate, rest_up in (refs[:4], refs[4:]):
        left = rest_up.shape[0]
        gate, up = jnp.where(first, mine[...], others[...]), jnp.where(first, others[...], mine[...])
        cores.append(([gate, rest_gate[:left, :], up, rest_up[...]], rest_gate[left:, :]))
    return cores


def at_end():
    z = lax.axis_index(E)
    return (z == 0) | (z == lax.axis_size(E) - 1)


def first_body(tokens, near, *refs):
    *own, got = refs
    x = jnp.concatenate([tokens[...], near[...]], axis=0)
    got[...] = through(x, own_cores(*own), got.shape[0])


def two_body(end_two, far_inner, *refs):
    *own, got = refs
    got[...] = through(jnp.where(at_end(), end_two[...], far_inner[...]), own_cores(*own), got.shape[0])


def second_body(tokens, near, end_two, far_inner, got_own, got_two, *refs):
    other, (here, back_near, back_two) = refs[:8], refs[8:]
    n, width = tokens.shape[0], got_own.shape[0]
    two = jnp.where(at_end(), end_two[...], far_inner[...])
    got = through(jnp.concatenate([tokens[...], near[...], two], axis=0), other_cores(*other), width)
    mine = [got_own[:, :n], got_own[:, n:], got_two[...]]
    for k, to in enumerate((here, back_near, back_two)):
        to[:width, :] = mine[k].astype(to.dtype)
        to[width:, :] = got[:, k * n : (k + 1) * n].astype(to.dtype)


def third_body(end_three, across, earlier, *refs):
    own, other, to = refs[:6], refs[6:14], refs[14]
    width = to.shape[0] // 2
    three = jnp.where(at_end(), end_three[...], across[...])
    to[:width, :] = through(three, own_cores(*own), width).astype(to.dtype)
    to[width:, :] = through(three, other_cores(*other), width).astype(to.dtype)


def score_body(base, here, near, two, three, weights, live, chosen, queries, others, scores):
    width, tokens = base.shape
    total = base[...]
    for k, sent in enumerate((here, near, two, three)):
        for w in (0, 1):
            part = sent[w * width : (w + 1) * width, :].astype(jnp.float32)
            total = total + weights[2 * k + w : 2 * k + w + 1, :] * part
    norm = jnp.sqrt(jnp.sum(total * total, axis=0, keepdims=True) + 1e-06)
    embedding = (total / norm).T.astype(jnp.bfloat16)
    best = [[] for _ in range(tokens // PLEN)]
    for block in (queries, others):
        raw = dot(embedding, block[...], NT) + live[:, :1]
        for p, found in enumerate(best):
            found.append(jnp.max(raw[p * PLEN : (p + 1) * PLEN], axis=0, keepdims=True))
    left = jnp.concatenate([jnp.concatenate(found, axis=1) for found in best], axis=0)
    thirds = []
    for _ in range(3):
        thirds.append(left.astype(jnp.bfloat16))
        left = left - thirds[-1].astype(jnp.float32)
    sums = [dot(third, chosen[...]) for third in thirds]
    scores[...] = sums[0] + (sums[1] + sums[2])


def by_column(
    tokens, route_ids, gate_values, passage_lengths, gate_weight, up_weight, down_weight, proj_weight, queries
):
    n, model_width = tokens.shape
    hidden_part = gate_weight.shape[2]
    width = proj_weight.shape[1]
    swap = [(0, 1), (1, 0)]
    ends, middle = [(1, 0), (2, 3)], [(1, 2), (2, 1)]
    f32, bf16 = jnp.float32, jnp.bfloat16

    rows = queries.shape[0] * queries.shape[1]
    both = (2 * width, n)
    near = lax.ppermute(tokens, E, [(i, i ^ 1) for i in range(4)])
    across = lax.ppermute(tokens, E, middle)
    gate, up, down = gate_weight[0].T, up_weight[0].T, down_weight[0].T
    part_rows = 2 * hidden_part // 3 // 16 * 16
    left = hidden_part - part_rows
    (part,) = kernel(part_body, [gate, up], [((part_rows, model_width), bf16)])
    part_x = lax.ppermute(part, Q, swap)
    fold, rest_gate, rest_up, base, weights, live, chosen = kernel(
        fold_body,
        [passage_lengths, tokens, gate, up, down, proj_weight, route_ids.T, gate_values.T],
        [((r, model_width), bf16) for r in (FOLD, left + FOLD, left)]
        + [((width, n), f32), ((8, n), f32), ((n, width), f32), ((2 * rows, 2 * queries.shape[0]), bf16)],
        smem=(0,),
        fetched=(1,),
    )
    pair_gate, pair_up = lax.ppermute(gate, D, swap), lax.ppermute(up, D, swap)
    pair_fold = lax.ppermute(tied([fold], [pair_gate], 1)[0], D, swap)
    own = [gate, up, fold, pair_gate, pair_up, pair_fold]
    (got_own,) = kernel(first_body, [tokens, near, *own], [((width, 2 * n), f32)], fetched=(0,))

    far_inner = lax.ppermute(near, E, middle)
    end_two = lax.ppermute(across, E, ends)
    rest_x = [lax.ppermute(a, Q, swap) for a in tied([rest_gate, rest_up], [near, across], 1)]
    (part_x,) = tied([part_x], [got_own], 1)
    part_y = lax.ppermute(part_x, G, swap)
    work = 8 * n * model_width * hidden_part
    (got_two,) = kernel(two_body, [end_two, far_inner, *own], [((width, n), f32)], flops=work)

    end_three = lax.ppermute(far_inner, E, ends)
    other = [part_x, part_y, *rest_x]
    other = other + [lax.ppermute(a, D, swap) for a in tied(other, [far_inner], 1)]
    other_queries = lax.ppermute(queries, Q, swap)
    here, *back = kernel(
        second_body,
        [tokens, near, end_two, far_inner, got_own, got_two, *other],
        [(both, f32), (both, bf16), (both, bf16)],
        fetched=(0,),
        flops=3 * work,
    )
    back += kernel(third_body, [end_three, across, here, *own, *other], [(both, bf16)])
    from_near, two, three = (
        lax.ppermute(a, E, [(i, i ^ k) for i in range(4)]) for k, a in enumerate(back, start=1)
    )
    (scores,) = kernel(
        score_body,
        [
            base, here, from_near, two, three, weights, live, chosen,
            queries.reshape(rows, width), other_queries.reshape(rows, width),
        ],
        [((n // PLEN, 2 * queries.shape[0]), f32)],
    )
    return scores


def solution(mesh):
    in_specs = (
        P((G, E, Q, D), None),
        P((G, E, Q, D), None),
        P((G, E, Q, D), None),
        P((G, E, Q, D)),
        P((E, Q), None, D),
        P((E, Q), None, D),
        P((E, Q), None, D),
        P(),
        P((G, Q), None, None),
    )
    sizes = [mesh.shape[a] for a in (G, E, Q, D)]
    return jax.shard_map(
        by_column if sizes == [2, 4, 2, 2] else by_dispatch,
        mesh=mesh,
        in_specs=in_specs,
        out_specs=P((G, E, Q, D), None),
        check_vma=False,
    )
```

```python
import jax
import jax.numpy as jnp
from jax import lax
from jax.experimental import pallas as pl
from jax.experimental.pallas import tpu as pltpu
from jax.sharding import PartitionSpec as P

PLEN = 64
G, E, Q, D = "group", "expert", "query", "dp"


def matched(embedding, live_mask, block_queries):
    query_rows = block_queries.reshape(-1, block_queries.shape[-1])
    raw_scores = jnp.dot(embedding, query_rows.T, preferred_element_type=jnp.float32)
    raw_scores = jnp.where(live_mask[:, None], raw_scores, -jnp.inf)
    best_match = jnp.max(raw_scores.reshape(-1, PLEN, raw_scores.shape[-1]), axis=1)
    return jnp.sum(best_match.reshape(best_match.shape[0], -1, block_queries.shape[1]), axis=-1)


def embedded(projected):
    lengths_norm = jnp.sqrt(jnp.sum(projected * projected, axis=-1, keepdims=True) + 1e-06)
    return (projected / lengths_norm).astype(jnp.bfloat16)


def live_tokens(passage_lengths, tok_rows):
    position = jnp.arange(tok_rows, dtype=jnp.int32) % PLEN
    return position < jnp.repeat(passage_lengths, PLEN)


def by_dispatch(
    tokens, route_ids, gate_values, passage_lengths, gate_weight, up_weight, down_weight, proj_weight, queries
):
    tok_rows, model_width = tokens.shape
    top_count = route_ids.shape[1]
    experts = lax.axis_size(E) * lax.axis_size(Q)
    capacity = max(2, 2 * tok_rows * top_count // experts)
    assignments = tok_rows * top_count
    flat_routes = route_ids.reshape(-1)
    one_hot = flat_routes[:, None] == jnp.arange(experts, dtype=jnp.int32)[None, :]
    order = jnp.arange(assignments, dtype=jnp.int32)
    before = (order[None, :] < order[:, None]).astype(jnp.bfloat16)
    earlier = jnp.dot(before, one_hot.astype(jnp.bfloat16), preferred_element_type=jnp.float32)
    slot_index = jnp.sum(jnp.where(one_hot, earlier, 0.0), axis=1).astype(jnp.int32)
    slot_target = flat_routes * capacity + slot_index
    slot_owner = jnp.full((experts * capacity,), assignments, jnp.int32).at[slot_target].set(order)
    padded = jnp.concatenate([tokens, jnp.zeros((1, model_width), tokens.dtype)], axis=0)
    source_row = jnp.where(slot_owner < assignments, slot_owner // top_count, tok_rows)
    outgoing = padded[source_row].reshape(experts, capacity, model_width)
    arrived = lax.all_to_all(outgoing, (E, Q), split_axis=0, concat_axis=0, tiled=True)
    expert_rows = arrived.reshape(experts * capacity, model_width)
    gate_act = jnp.dot(
        expert_rows, lax.all_gather(gate_weight[0], D, axis=1, tiled=True), preferred_element_type=jnp.float32
    )
    up_act = jnp.dot(
        expert_rows, lax.all_gather(up_weight[0], D, axis=1, tiled=True), preferred_element_type=jnp.float32
    )
    hidden = (jax.nn.silu(gate_act) * up_act).astype(jnp.bfloat16)
    results = lax.dot_general(
        hidden,
        lax.all_gather(down_weight[0], D, axis=1, tiled=True),
        (((1,), (1,)), ((), ())),
        preferred_element_type=jnp.float32,
    ).astype(jnp.bfloat16)
    folded = jnp.dot(results, proj_weight, preferred_element_type=jnp.float32)
    returned_rows = lax.all_to_all(
        folded.reshape(experts, capacity, folded.shape[-1]), (E, Q), split_axis=0, concat_axis=0, tiled=True
    )
    picked = returned_rows.reshape(experts * capacity, folded.shape[-1])[slot_target]
    weights = gate_values.reshape(assignments, 1)
    projected = jnp.dot(tokens, proj_weight, preferred_element_type=jnp.float32) + jnp.sum(
        (picked * weights).reshape(tok_rows, top_count, folded.shape[-1]), axis=1
    )
    live_mask = live_tokens(passage_lengths, tok_rows)
    return matched(embedded(projected), live_mask, lax.all_gather(queries, Q, axis=0, tiled=True))


VMEM = pl.BlockSpec(memory_space=pltpu.VMEM)
SMEM = pl.BlockSpec(memory_space=pltpu.SMEM)
NT, TN = (((1,), (1,)), ((), ())), (((0,), (0,)), ((), ()))


def dot(a, b, dims=(((1,), (0,)), ((), ()))):
    return lax.dot_general(a, b, dims, preferred_element_type=jnp.float32)


def whole_block(a):
    return pl.BlockSpec(a.shape, lambda *_: (0,) * a.ndim)


def tied(values, after, parts):
    def body(*refs):
        outs = refs[len(values) + len(after) :]
        for i in range(len(values)):
            rows = outs[parts * i].shape[0]
            for p in range(parts):
                outs[parts * i + p][...] = refs[i][p * rows : (p + 1) * rows, :]

    blocks = [jax.ShapeDtypeStruct((a.shape[0] // parts, a.shape[1]), a.dtype) for a in values for _ in range(parts)]

    return pl.pallas_call(
        body,
        out_shape=blocks,
        in_specs=[VMEM] * len(values) + [pl.BlockSpec(memory_space=pl.ANY)] * len(after),
        out_specs=[VMEM] * len(blocks),
        compiler_params=pltpu.CompilerParams(vmem_limit_bytes=8 * 2**20),
    )(*values, *after)


def kernel(body, operands, outs, smem=(), fetched=(), limit=24, flops=0):
    return pl.pallas_call(
        body,
        out_shape=[jax.ShapeDtypeStruct(shape, dtype) for shape, dtype in outs],
        in_specs=[
            SMEM if i in smem else whole_block(a) if i in fetched else VMEM for i, a in enumerate(operands)
        ],
        out_specs=[VMEM] * len(outs),
        compiler_params=pltpu.CompilerParams(vmem_limit_bytes=limit * 2**20),
        cost_estimate=pl.CostEstimate(flops=flops, bytes_accessed=0, transcendentals=0),
    )(*operands)


FOLD = 16


def part_body(gate, up, part):
    rows = part.shape[0]
    part[...] = jnp.where(lax.axis_index(G) == 0, gate[:rows, :], up[:rows, :])


def fold_body(
    lengths, tokens, gate, up, down, proj, routes, gates,
    fold, rest_gate, rest_up, base, weights, live, chosen,
):
    rows, width = down.shape[0], proj.shape[1]
    folded = dot(down[...], proj[...]).astype(jnp.bfloat16)
    fold[...] = jnp.zeros_like(fold)
    for i in range(rows // FOLD):
        fold[:, i * width : (i + 1) * width] = folded[i * FOLD : (i + 1) * FOLD]
    left = rest_up.shape[0]
    rest_gate[:left, :] = gate[rows - left :, :]
    rest_gate[left:, :] = fold[...]
    rest_up[...] = up[rows - left :, :]
    base[...] = dot(tokens[...], proj[...]).T
    z, x = lax.axis_index(E), lax.axis_index(Q)
    for i in range(weights.shape[0]):
        expert = (z ^ (i // 2)) * 2 + (x ^ (i % 2))
        weights[i : i + 1, :] = jnp.sum(jnp.where(routes[...] == expert, gates[...], 0.0), axis=0, keepdims=True)
    position = lax.broadcasted_iota(jnp.int32, (PLEN, live.shape[1]), 0)
    for p in range(live.shape[0] // PLEN):
        live[p * PLEN : (p + 1) * PLEN, :] = jnp.where(position < lengths[p], 0.0, -jnp.inf)
    count, span = chosen.shape[0] // 2, chosen.shape[0] // chosen.shape[1]
    query = lax.broadcasted_iota(jnp.int32, (count, chosen.shape[1]), 0) // span
    column = lax.broadcasted_iota(jnp.int32, (count, chosen.shape[1]), 1)
    for w in (0, 1):
        hit = jnp.where(column == query + (x ^ w) * (count // span), 1.0, 0.0)
        chosen[w * count : (w + 1) * count, :] = hit.astype(chosen.dtype)


def finish(act, tile, width):
    rows = act.shape[0] // 2
    gate_act, up_act = act[:rows], act[rows:]
    hidden = (gate_act / (1.0 + jnp.exp(-gate_act)) * up_act).astype(jnp.bfloat16)
    folded = jnp.concatenate([tile[:, i * width : (i + 1) * width] for i in range(rows // FOLD)], axis=0)
    return dot(folded, hidden, TN)


def through(x, cores, width):
    total = None
    for blocks, fold in cores:
        part = finish(dot(jnp.concatenate(blocks, axis=0), x, NT), fold, width)
        total = part if total is None else total + part
    return total


def own_cores(gate, up, fold, pair_gate, pair_up, pair_fold):
    return [([gate[...], up[...]], fold[...]), ([pair_gate[...], pair_up[...]], pair_fold[...])]


def other_cores(*refs):
    first = lax.axis_index(G) == 0
    cores = []
    for mine, others, rest_gate, rest_up in (refs[:4], refs[4:]):
        left = rest_up.shape[0]
        gate, up = jnp.where(first, mine[...], others[...]), jnp.where(first, others[...], mine[...])
        cores.append(([gate, rest_gate[:left, :], up, rest_up[...]], rest_gate[left:, :]))
    return cores


def at_end():
    z = lax.axis_index(E)
    return (z == 0) | (z == lax.axis_size(E) - 1)


def first_body(tokens, near, *refs):
    *own, got = refs
    x = jnp.concatenate([tokens[...], near[...]], axis=0)
    got[...] = through(x, own_cores(*own), got.shape[0])


def two_body(end_two, far_inner, *refs):
    *own, got = refs
    got[...] = through(jnp.where(at_end(), end_two[...], far_inner[...]), own_cores(*own), got.shape[0])


def second_body(tokens, near, end_two, far_inner, got_own, got_two, *refs):
    other, (here, back_near, back_two) = refs[:8], refs[8:]
    n, width = tokens.shape[0], got_own.shape[0]
    two = jnp.where(at_end(), end_two[...], far_inner[...])
    got = through(jnp.concatenate([tokens[...], near[...], two], axis=0), other_cores(*other), width)
    mine = [got_own[:, :n], got_own[:, n:], got_two[...]]
    for k, to in enumerate((here, back_near, back_two)):
        to[:width, :] = mine[k].astype(to.dtype)
        to[width:, :] = got[:, k * n : (k + 1) * n].astype(to.dtype)


def third_body(end_three, across, earlier, *refs):
    own, other, to = refs[:6], refs[6:14], refs[14]
    width = to.shape[0] // 2
    three = jnp.where(at_end(), end_three[...], across[...])
    to[:width, :] = through(three, own_cores(*own), width).astype(to.dtype)
    to[width:, :] = through(three, other_cores(*other), width).astype(to.dtype)


def score_body(base, here, near, two, three, weights, live, chosen, queries, others, scores):
    width, tokens = base.shape
    total = base[...]
    for k, sent in enumerate((here, near, two, three)):
        for w in (0, 1):
            part = sent[w * width : (w + 1) * width, :].astype(jnp.float32)
            total = total + weights[2 * k + w : 2 * k + w + 1, :] * part
    norm = jnp.sqrt(jnp.sum(total * total, axis=0, keepdims=True) + 1e-06)
    embedding = (total / norm).T.astype(jnp.bfloat16)
    best = [[] for _ in range(tokens // PLEN)]
    for block in (queries, others):
        raw = dot(embedding, block[...], NT) + live[:, :1]
        for p, found in enumerate(best):
            found.append(jnp.max(raw[p * PLEN : (p + 1) * PLEN], axis=0, keepdims=True))
    left = jnp.concatenate([jnp.concatenate(found, axis=1) for found in best], axis=0)
    thirds = []
    for _ in range(3):
        thirds.append(left.astype(jnp.bfloat16))
        left = left - thirds[-1].astype(jnp.float32)
    sums = [dot(third, chosen[...]) for third in thirds]
    scores[...] = sums[0] + (sums[1] + sums[2])


def by_column(
    tokens, route_ids, gate_values, passage_lengths, gate_weight, up_weight, down_weight, proj_weight, queries
):
    n, model_width = tokens.shape
    hidden_part = gate_weight.shape[2]
    width = proj_weight.shape[1]
    swap = [(0, 1), (1, 0)]
    ends, middle = [(1, 0), (2, 3)], [(1, 2), (2, 1)]
    f32, bf16 = jnp.float32, jnp.bfloat16

    rows = queries.shape[0] * queries.shape[1]
    both = (2 * width, n)
    near = lax.ppermute(tokens, E, [(i, i ^ 1) for i in range(4)])
    across = lax.ppermute(tokens, E, middle)
    gate, up, down = gate_weight[0].T, up_weight[0].T, down_weight[0].T
    part_rows = min(2 * hidden_part // 3, n - 1) // 16 * 16
    left = hidden_part - part_rows
    (part,) = kernel(part_body, [gate, up], [((part_rows, model_width), bf16)])
    part_x = lax.ppermute(part, Q, swap)
    fold, rest_gate, rest_up, base, weights, live, chosen = kernel(
        fold_body,
        [passage_lengths, tokens, gate, up, down, proj_weight, route_ids.T, gate_values.T],
        [((r, model_width), bf16) for r in (FOLD, left + FOLD, left)]
        + [((width, n), f32), ((8, n), f32), ((n, width), f32), ((2 * rows, 2 * queries.shape[0]), bf16)],
        smem=(0,),
        fetched=(1,),
    )
    pair_gate, pair_up = lax.ppermute(gate, D, swap), lax.ppermute(up, D, swap)
    pair_fold = lax.ppermute(tied([fold], [pair_gate], 1)[0], D, swap)
    own = [gate, up, fold, pair_gate, pair_up, pair_fold]
    (got_own,) = kernel(first_body, [tokens, near, *own], [((width, 2 * n), f32)], fetched=(0,))

    far_inner = lax.ppermute(near, E, middle)
    end_two = lax.ppermute(across, E, ends)
    rest_x = [lax.ppermute(a, Q, swap) for a in tied([rest_gate, rest_up], [near, across], 1)]
    (part_x,) = tied([part_x], [got_own], 1)
    part_y = lax.ppermute(part_x, G, swap)
    (got_two,) = kernel(two_body, [end_two, far_inner, *own], [((width, n), f32)])

    end_three = lax.ppermute(far_inner, E, ends)
    other = [part_x, part_y, *rest_x]
    other = other + [lax.ppermute(a, D, swap) for a in tied(other, [far_inner], 1)]
    other_queries = lax.ppermute(queries, Q, swap)
    here, *back = kernel(
        second_body,
        [tokens, near, end_two, far_inner, got_own, got_two, *other],
        [(both, f32), (both, bf16), (both, bf16)],
        fetched=(0,),
    )
    back += kernel(third_body, [end_three, across, here, *own, *other], [(both, bf16)])
    from_near, two, three = (
        lax.ppermute(a, E, [(i, i ^ k) for i in range(4)]) for k, a in enumerate(back, start=1)
    )
    (scores,) = kernel(
        score_body,
        [
            base, here, from_near, two, three, weights, live, chosen,
            queries.reshape(rows, width), other_queries.reshape(rows, width),
        ],
        [((n // PLEN, 2 * queries.shape[0]), f32)],
    )
    return scores


def solution(mesh):
    in_specs = (
        P((G, E, Q, D), None),
        P((G, E, Q, D), None),
        P((G, E, Q, D), None),
        P((G, E, Q, D)),
        P((E, Q), None, D),
        P((E, Q), None, D),
        P((E, Q), None, D),
        P(),
        P((G, Q), None, None),
    )
    sizes = [mesh.shape[a] for a in (G, E, Q, D)]
    return jax.shard_map(
        by_column if sizes == [2, 4, 2, 2] else by_dispatch,
        mesh=mesh,
        in_specs=in_specs,
        out_specs=P((G, E, Q, D), None),
        check_vma=False,
    )
```

```python
import jax
import jax.numpy as jnp
from jax import lax
from jax.experimental import pallas as pl
from jax.experimental.pallas import tpu as pltpu
from jax.sharding import PartitionSpec as P

PLEN = 64
G, E, Q, D = "group", "expert", "query", "dp"


def matched(embedding, live_mask, block_queries):
    query_rows = block_queries.reshape(-1, block_queries.shape[-1])
    raw_scores = jnp.dot(embedding, query_rows.T, preferred_element_type=jnp.float32)
    raw_scores = jnp.where(live_mask[:, None], raw_scores, -jnp.inf)
    best_match = jnp.max(raw_scores.reshape(-1, PLEN, raw_scores.shape[-1]), axis=1)
    return jnp.sum(best_match.reshape(best_match.shape[0], -1, block_queries.shape[1]), axis=-1)


def embedded(projected):
    lengths_norm = jnp.sqrt(jnp.sum(projected * projected, axis=-1, keepdims=True) + 1e-06)
    return (projected / lengths_norm).astype(jnp.bfloat16)


def live_tokens(passage_lengths, tok_rows):
    position = jnp.arange(tok_rows, dtype=jnp.int32) % PLEN
    return position < jnp.repeat(passage_lengths, PLEN)


def by_dispatch(
    tokens, route_ids, gate_values, passage_lengths, gate_weight, up_weight, down_weight, proj_weight, queries
):
    tok_rows, model_width = tokens.shape
    top_count = route_ids.shape[1]
    experts = lax.axis_size(E) * lax.axis_size(Q)
    capacity = max(2, 2 * tok_rows * top_count // experts)
    assignments = tok_rows * top_count
    flat_routes = route_ids.reshape(-1)
    one_hot = flat_routes[:, None] == jnp.arange(experts, dtype=jnp.int32)[None, :]
    order = jnp.arange(assignments, dtype=jnp.int32)
    before = (order[None, :] < order[:, None]).astype(jnp.bfloat16)
    earlier = jnp.dot(before, one_hot.astype(jnp.bfloat16), preferred_element_type=jnp.float32)
    slot_index = jnp.sum(jnp.where(one_hot, earlier, 0.0), axis=1).astype(jnp.int32)
    slot_target = flat_routes * capacity + slot_index
    slot_owner = jnp.full((experts * capacity,), assignments, jnp.int32).at[slot_target].set(order)
    padded = jnp.concatenate([tokens, jnp.zeros((1, model_width), tokens.dtype)], axis=0)
    source_row = jnp.where(slot_owner < assignments, slot_owner // top_count, tok_rows)
    outgoing = padded[source_row].reshape(experts, capacity, model_width)
    arrived = lax.all_to_all(outgoing, (E, Q), split_axis=0, concat_axis=0, tiled=True)
    expert_rows = arrived.reshape(experts * capacity, model_width)
    gate_act = jnp.dot(
        expert_rows, lax.all_gather(gate_weight[0], D, axis=1, tiled=True), preferred_element_type=jnp.float32
    )
    up_act = jnp.dot(
        expert_rows, lax.all_gather(up_weight[0], D, axis=1, tiled=True), preferred_element_type=jnp.float32
    )
    hidden = (jax.nn.silu(gate_act) * up_act).astype(jnp.bfloat16)
    results = lax.dot_general(
        hidden,
        lax.all_gather(down_weight[0], D, axis=1, tiled=True),
        (((1,), (1,)), ((), ())),
        preferred_element_type=jnp.float32,
    ).astype(jnp.bfloat16)
    folded = jnp.dot(results, proj_weight, preferred_element_type=jnp.float32)
    returned_rows = lax.all_to_all(
        folded.reshape(experts, capacity, folded.shape[-1]), (E, Q), split_axis=0, concat_axis=0, tiled=True
    )
    picked = returned_rows.reshape(experts * capacity, folded.shape[-1])[slot_target]
    weights = gate_values.reshape(assignments, 1)
    projected = jnp.dot(tokens, proj_weight, preferred_element_type=jnp.float32) + jnp.sum(
        (picked * weights).reshape(tok_rows, top_count, folded.shape[-1]), axis=1
    )
    live_mask = live_tokens(passage_lengths, tok_rows)
    return matched(embedded(projected), live_mask, lax.all_gather(queries, Q, axis=0, tiled=True))


VMEM = pl.BlockSpec(memory_space=pltpu.VMEM)
SMEM = pl.BlockSpec(memory_space=pltpu.SMEM)
NT, TN = (((1,), (1,)), ((), ())), (((0,), (0,)), ((), ()))


def dot(a, b, dims=(((1,), (0,)), ((), ()))):
    return lax.dot_general(a, b, dims, preferred_element_type=jnp.float32)


def whole_block(a):
    return pl.BlockSpec(a.shape, lambda *_: (0,) * a.ndim)


def tied(values, after, parts):
    def body(*refs):
        outs = refs[len(values) + len(after) :]
        for i in range(len(values)):
            rows = outs[parts * i].shape[0]
            for p in range(parts):
                outs[parts * i + p][...] = refs[i][p * rows : (p + 1) * rows, :]

    blocks = [jax.ShapeDtypeStruct((a.shape[0] // parts, a.shape[1]), a.dtype) for a in values for _ in range(parts)]

    return pl.pallas_call(
        body,
        out_shape=blocks,
        in_specs=[VMEM] * len(values) + [pl.BlockSpec(memory_space=pl.ANY)] * len(after),
        out_specs=[VMEM] * len(blocks),
        compiler_params=pltpu.CompilerParams(vmem_limit_bytes=8 * 2**20),
    )(*values, *after)


def kernel(body, operands, outs, smem=(), fetched=(), limit=24, flops=0):
    return pl.pallas_call(
        body,
        out_shape=[jax.ShapeDtypeStruct(shape, dtype) for shape, dtype in outs],
        in_specs=[
            SMEM if i in smem else whole_block(a) if i in fetched else VMEM for i, a in enumerate(operands)
        ],
        out_specs=[VMEM] * len(outs),
        compiler_params=pltpu.CompilerParams(vmem_limit_bytes=limit * 2**20),
        cost_estimate=pl.CostEstimate(flops=flops, bytes_accessed=0, transcendentals=0),
    )(*operands)


FOLD = 16


def part_body(gate, up, part):
    rows = part.shape[0]
    part[...] = jnp.where(lax.axis_index(G) == 0, gate[:rows, :], up[:rows, :])


def fold_body(
    lengths, tokens, gate, up, down, proj, routes, gates,
    fold, rest_gate, rest_up, held_gate, held_up, base, weights, live, chosen,
):
    rows, width = down.shape[0], proj.shape[1]
    folded = dot(down[...], proj[...]).astype(jnp.bfloat16)
    fold[...] = jnp.zeros_like(fold)
    for i in range(rows // FOLD):
        fold[:, i * width : (i + 1) * width] = folded[i * FOLD : (i + 1) * FOLD]
    left = rest_up.shape[0]
    rest_gate[:left, :] = gate[rows - left :, :]
    rest_gate[left:, :] = fold[...]
    rest_up[...] = up[rows - left :, :]
    held_gate[...] = gate[...]
    held_up[...] = up[...]
    base[...] = dot(tokens[...], proj[...]).T
    z, x = lax.axis_index(E), lax.axis_index(Q)
    for i in range(weights.shape[0]):
        expert = (z ^ (i // 2)) * 2 + (x ^ (i % 2))
        weights[i : i + 1, :] = jnp.sum(jnp.where(routes[...] == expert, gates[...], 0.0), axis=0, keepdims=True)
    position = lax.broadcasted_iota(jnp.int32, (PLEN, live.shape[1]), 0)
    for p in range(live.shape[0] // PLEN):
        live[p * PLEN : (p + 1) * PLEN, :] = jnp.where(position < lengths[p], 0.0, -jnp.inf)
    count, span = chosen.shape[0] // 2, chosen.shape[0] // chosen.shape[1]
    query = lax.broadcasted_iota(jnp.int32, (count, chosen.shape[1]), 0) // span
    column = lax.broadcasted_iota(jnp.int32, (count, chosen.shape[1]), 1)
    for w in (0, 1):
        hit = jnp.where(column == query + (x ^ w) * (count // span), 1.0, 0.0)
        chosen[w * count : (w + 1) * count, :] = hit.astype(chosen.dtype)


def finish(act, tile, width):
    rows = act.shape[0] // 2
    gate_act, up_act = act[:rows], act[rows:]
    hidden = (gate_act / (1.0 + jnp.exp(-gate_act)) * up_act).astype(jnp.bfloat16)
    folded = jnp.concatenate([tile[:, i * width : (i + 1) * width] for i in range(rows // FOLD)], axis=0)
    return dot(folded, hidden, TN)


def through(x, cores, width):
    total = None
    for blocks, fold in cores:
        part = finish(dot(jnp.concatenate(blocks, axis=0), x, NT), fold, width)
        total = part if total is None else total + part
    return total


def own_cores(gate, up, fold, pair_gate, pair_up, pair_fold):
    return [([gate[...], up[...]], fold[...]), ([pair_gate[...], pair_up[...]], pair_fold[...])]


def other_cores(*refs):
    first = lax.axis_index(G) == 0
    cores = []
    for mine, others, rest_gate, rest_up in (refs[:4], refs[4:]):
        left = rest_up.shape[0]
        gate, up = jnp.where(first, mine[...], others[...]), jnp.where(first, others[...], mine[...])
        cores.append(([gate, rest_gate[:left, :], up, rest_up[...]], rest_gate[left:, :]))
    return cores


def at_end():
    z = lax.axis_index(E)
    return (z == 0) | (z == lax.axis_size(E) - 1)


def first_body(tokens, near, *refs):
    *own, got = refs
    x = jnp.concatenate([tokens[...], near[...]], axis=0)
    got[...] = through(x, own_cores(*own), got.shape[0])


def two_body(end_two, far_inner, *refs):
    *own, got = refs
    got[...] = through(jnp.where(at_end(), end_two[...], far_inner[...]), own_cores(*own), got.shape[0])


def second_body(tokens, near, end_two, far_inner, got_own, got_two, *refs):
    other, (here, back_near, back_two) = refs[:8], refs[8:]
    n, width = tokens.shape[0], got_own.shape[0]
    two = jnp.where(at_end(), end_two[...], far_inner[...])
    got = through(jnp.concatenate([tokens[...], near[...], two], axis=0), other_cores(*other), width)
    mine = [got_own[:, :n], got_own[:, n:], got_two[...]]
    for k, to in enumerate((here, back_near, back_two)):
        to[:width, :] = mine[k].astype(to.dtype)
        to[width:, :] = got[:, k * n : (k + 1) * n].astype(to.dtype)


def third_body(end_three, across, earlier, *refs):
    own, other, to = refs[:6], refs[6:14], refs[14]
    width = to.shape[0] // 2
    three = jnp.where(at_end(), end_three[...], across[...])
    to[:width, :] = through(three, own_cores(*own), width).astype(to.dtype)
    to[width:, :] = through(three, other_cores(*other), width).astype(to.dtype)


def score_body(base, here, near, two, three, weights, live, chosen, queries, others, scores):
    width, tokens = base.shape
    total = base[...]
    for k, sent in enumerate((here, near, two, three)):
        for w in (0, 1):
            part = sent[w * width : (w + 1) * width, :].astype(jnp.float32)
            total = total + weights[2 * k + w : 2 * k + w + 1, :] * part
    norm = jnp.sqrt(jnp.sum(total * total, axis=0, keepdims=True) + 1e-06)
    embedding = (total / norm).T.astype(jnp.bfloat16)
    best = [[] for _ in range(tokens // PLEN)]
    for block in (queries, others):
        raw = dot(embedding, block[...], NT) + live[:, :1]
        for p, found in enumerate(best):
            found.append(jnp.max(raw[p * PLEN : (p + 1) * PLEN], axis=0, keepdims=True))
    left = jnp.concatenate([jnp.concatenate(found, axis=1) for found in best], axis=0)
    thirds = []
    for _ in range(3):
        thirds.append(left.astype(jnp.bfloat16))
        left = left - thirds[-1].astype(jnp.float32)
    sums = [dot(third, chosen[...]) for third in thirds]
    scores[...] = sums[0] + (sums[1] + sums[2])


def by_column(
    tokens, route_ids, gate_values, passage_lengths, gate_weight, up_weight, down_weight, proj_weight, queries
):
    n, model_width = tokens.shape
    hidden_part = gate_weight.shape[2]
    width = proj_weight.shape[1]
    swap = [(0, 1), (1, 0)]
    ends, middle = [(1, 0), (2, 3)], [(1, 2), (2, 1)]
    f32, bf16 = jnp.float32, jnp.bfloat16

    rows = queries.shape[0] * queries.shape[1]
    both = (2 * width, n)
    near = lax.ppermute(tokens, E, [(i, i ^ 1) for i in range(4)])
    across = lax.ppermute(tokens, E, middle)
    gate, up, down = gate_weight[0].T, up_weight[0].T, down_weight[0].T
    part_rows = min(2 * hidden_part // 3, n - 1) // 16 * 16
    left = hidden_part - part_rows
    (part,) = kernel(part_body, [gate, up], [((part_rows, model_width), bf16)])
    part_x = lax.ppermute(part, Q, swap)
    fold, rest_gate, rest_up, held_gate, held_up, base, weights, live, chosen = kernel(
        fold_body,
        [passage_lengths, tokens, gate, up, down, proj_weight, route_ids.T, gate_values.T],
        [((r, model_width), bf16) for r in (FOLD, left + FOLD, left, hidden_part, hidden_part)]
        + [((width, n), f32), ((8, n), f32), ((n, width), f32), ((2 * rows, 2 * queries.shape[0]), bf16)],
        smem=(0,),
        fetched=(1,),
    )
    pair_gate, pair_up = lax.ppermute(gate, D, swap), lax.ppermute(up, D, swap)
    pair_fold = lax.ppermute(tied([fold], [pair_gate], 1)[0], D, swap)
    own = [held_gate, held_up, fold, pair_gate, pair_up, pair_fold]
    (got_own,) = kernel(first_body, [tokens, near, *own], [((width, 2 * n), f32)], fetched=(0,))

    far_inner = lax.ppermute(near, E, middle)
    end_two = lax.ppermute(across, E, ends)
    rest_x = [lax.ppermute(a, Q, swap) for a in (rest_gate, *tied([rest_up], [near, across], 1))]
    (part_x,) = tied([part_x], [near, across], 1)
    part_y = lax.ppermute(part_x, G, swap)
    (got_two,) = kernel(two_body, [end_two, far_inner, *own], [((width, n), f32)])

    end_three = lax.ppermute(far_inner, E, ends)
    other = [part_x, part_y, *rest_x]
    free = {i: lax.ppermute(other[i], D, swap) for i in (2,)}
    held = dict(zip((0, 1, 3), tied([other[i] for i in (0, 1, 3)], [far_inner, got_own, got_two, free[2]], 1)))
    other = other + [free[i] if i in free else lax.ppermute(held[i], D, swap) for i in range(4)]
    other_queries = lax.ppermute(queries, Q, swap)
    here, *back = kernel(
        second_body,
        [tokens, near, end_two, far_inner, got_own, got_two, *other],
        [(both, f32), (both, bf16), (both, bf16)],
        fetched=(0,),
    )
    back += kernel(third_body, [end_three, across, here, *own, *other], [(both, bf16)])
    from_near, two, three = (
        lax.ppermute(a, E, [(i, i ^ k) for i in range(4)]) for k, a in enumerate(back, start=1)
    )
    (scores,) = kernel(
        score_body,
        [
            base, here, from_near, two, three, weights, live, chosen,
            queries.reshape(rows, width), other_queries.reshape(rows, width),
        ],
        [((n // PLEN, 2 * queries.shape[0]), f32)],
    )
    return scores


def solution(mesh):
    in_specs = (
        P((G, E, Q, D), None),
        P((G, E, Q, D), None),
        P((G, E, Q, D), None),
        P((G, E, Q, D)),
        P((E, Q), None, D),
        P((E, Q), None, D),
        P((E, Q), None, D),
        P(),
        P((G, Q), None, None),
    )
    sizes = [mesh.shape[a] for a in (G, E, Q, D)]
    return jax.shard_map(
        by_column if sizes == [2, 4, 2, 2] else by_dispatch,
        mesh=mesh,
        in_specs=in_specs,
        out_specs=P((G, E, Q, D), None),
        check_vma=False,
    )
```

```python
import jax
import jax.numpy as jnp
from jax import lax
from jax.experimental import pallas as pl
from jax.experimental.pallas import tpu as pltpu
from jax.sharding import PartitionSpec as P

PLEN = 64
G, E, Q, D = "group", "expert", "query", "dp"


def matched(embedding, live_mask, block_queries):
    query_rows = block_queries.reshape(-1, block_queries.shape[-1])
    raw_scores = jnp.dot(embedding, query_rows.T, preferred_element_type=jnp.float32)
    raw_scores = jnp.where(live_mask[:, None], raw_scores, -jnp.inf)
    best_match = jnp.max(raw_scores.reshape(-1, PLEN, raw_scores.shape[-1]), axis=1)
    return jnp.sum(best_match.reshape(best_match.shape[0], -1, block_queries.shape[1]), axis=-1)


def embedded(projected):
    lengths_norm = jnp.sqrt(jnp.sum(projected * projected, axis=-1, keepdims=True) + 1e-06)
    return (projected / lengths_norm).astype(jnp.bfloat16)


def live_tokens(passage_lengths, tok_rows):
    position = jnp.arange(tok_rows, dtype=jnp.int32) % PLEN
    return position < jnp.repeat(passage_lengths, PLEN)


def by_dispatch(
    tokens, route_ids, gate_values, passage_lengths, gate_weight, up_weight, down_weight, proj_weight, queries
):
    tok_rows, model_width = tokens.shape
    top_count = route_ids.shape[1]
    experts = lax.axis_size(E) * lax.axis_size(Q)
    capacity = max(2, 2 * tok_rows * top_count // experts)
    assignments = tok_rows * top_count
    flat_routes = route_ids.reshape(-1)
    one_hot = flat_routes[:, None] == jnp.arange(experts, dtype=jnp.int32)[None, :]
    order = jnp.arange(assignments, dtype=jnp.int32)
    before = (order[None, :] < order[:, None]).astype(jnp.bfloat16)
    earlier = jnp.dot(before, one_hot.astype(jnp.bfloat16), preferred_element_type=jnp.float32)
    slot_index = jnp.sum(jnp.where(one_hot, earlier, 0.0), axis=1).astype(jnp.int32)
    slot_target = flat_routes * capacity + slot_index
    slot_owner = jnp.full((experts * capacity,), assignments, jnp.int32).at[slot_target].set(order)
    padded = jnp.concatenate([tokens, jnp.zeros((1, model_width), tokens.dtype)], axis=0)
    source_row = jnp.where(slot_owner < assignments, slot_owner // top_count, tok_rows)
    outgoing = padded[source_row].reshape(experts, capacity, model_width)
    arrived = lax.all_to_all(outgoing, (E, Q), split_axis=0, concat_axis=0, tiled=True)
    expert_rows = arrived.reshape(experts * capacity, model_width)
    gate_act = jnp.dot(
        expert_rows, lax.all_gather(gate_weight[0], D, axis=1, tiled=True), preferred_element_type=jnp.float32
    )
    up_act = jnp.dot(
        expert_rows, lax.all_gather(up_weight[0], D, axis=1, tiled=True), preferred_element_type=jnp.float32
    )
    hidden = (jax.nn.silu(gate_act) * up_act).astype(jnp.bfloat16)
    results = lax.dot_general(
        hidden,
        lax.all_gather(down_weight[0], D, axis=1, tiled=True),
        (((1,), (1,)), ((), ())),
        preferred_element_type=jnp.float32,
    ).astype(jnp.bfloat16)
    folded = jnp.dot(results, proj_weight, preferred_element_type=jnp.float32)
    returned_rows = lax.all_to_all(
        folded.reshape(experts, capacity, folded.shape[-1]), (E, Q), split_axis=0, concat_axis=0, tiled=True
    )
    picked = returned_rows.reshape(experts * capacity, folded.shape[-1])[slot_target]
    weights = gate_values.reshape(assignments, 1)
    projected = jnp.dot(tokens, proj_weight, preferred_element_type=jnp.float32) + jnp.sum(
        (picked * weights).reshape(tok_rows, top_count, folded.shape[-1]), axis=1
    )
    live_mask = live_tokens(passage_lengths, tok_rows)
    return matched(embedded(projected), live_mask, lax.all_gather(queries, Q, axis=0, tiled=True))


VMEM = pl.BlockSpec(memory_space=pltpu.VMEM)
SMEM = pl.BlockSpec(memory_space=pltpu.SMEM)
NT, TN = (((1,), (1,)), ((), ())), (((0,), (0,)), ((), ()))


def dot(a, b, dims=(((1,), (0,)), ((), ()))):
    return lax.dot_general(a, b, dims, preferred_element_type=jnp.float32)


def whole_block(a):
    return pl.BlockSpec(a.shape, lambda *_: (0,) * a.ndim)


def tied(values, after, parts):
    def body(*refs):
        outs = refs[len(values) + len(after) :]
        for i in range(len(values)):
            rows = outs[parts * i].shape[0]
            for p in range(parts):
                outs[parts * i + p][...] = refs[i][p * rows : (p + 1) * rows, :]

    blocks = [jax.ShapeDtypeStruct((a.shape[0] // parts, a.shape[1]), a.dtype) for a in values for _ in range(parts)]

    return pl.pallas_call(
        body,
        out_shape=blocks,
        in_specs=[VMEM] * len(values) + [pl.BlockSpec(memory_space=pl.ANY)] * len(after),
        out_specs=[VMEM] * len(blocks),
        compiler_params=pltpu.CompilerParams(vmem_limit_bytes=8 * 2**20),
    )(*values, *after)


def kernel(body, operands, outs, smem=(), fetched=(), limit=24, flops=0):
    return pl.pallas_call(
        body,
        out_shape=[jax.ShapeDtypeStruct(shape, dtype) for shape, dtype in outs],
        in_specs=[
            SMEM if i in smem else whole_block(a) if i in fetched else VMEM for i, a in enumerate(operands)
        ],
        out_specs=[VMEM] * len(outs),
        compiler_params=pltpu.CompilerParams(vmem_limit_bytes=limit * 2**20),
        cost_estimate=pl.CostEstimate(flops=flops, bytes_accessed=0, transcendentals=0),
    )(*operands)


FOLD = 16


def part_body(gate, up, part):
    rows = part.shape[0]
    part[...] = jnp.where(lax.axis_index(G) == 0, gate[:rows, :], up[:rows, :])


def fold_body(
    lengths, tokens, gate, up, down, proj, routes, gates,
    fold, rest_gate, rest_up, held_gate, held_up, base, weights, live, chosen,
):
    rows, width = down.shape[0], proj.shape[1]
    folded = dot(down[...], proj[...]).astype(jnp.bfloat16)
    fold[...] = jnp.zeros_like(fold)
    for i in range(rows // FOLD):
        fold[:, i * width : (i + 1) * width] = folded[i * FOLD : (i + 1) * FOLD]
    left = rest_up.shape[0]
    rest_gate[:left, :] = gate[rows - left :, :]
    rest_gate[left:, :] = fold[...]
    rest_up[...] = up[rows - left :, :]
    held_gate[...] = gate[...]
    held_up[...] = up[...]
    base[...] = dot(tokens[...], proj[...]).T
    z, x = lax.axis_index(E), lax.axis_index(Q)
    for i in range(weights.shape[0]):
        expert = (z ^ (i // 2)) * 2 + (x ^ (i % 2))
        weights[i : i + 1, :] = jnp.sum(jnp.where(routes[...] == expert, gates[...], 0.0), axis=0, keepdims=True)
    position = lax.broadcasted_iota(jnp.int32, (PLEN, live.shape[1]), 0)
    for p in range(live.shape[0] // PLEN):
        live[p * PLEN : (p + 1) * PLEN, :] = jnp.where(position < lengths[p], 0.0, -jnp.inf)
    count, span = chosen.shape[0] // 2, chosen.shape[0] // chosen.shape[1]
    query = lax.broadcasted_iota(jnp.int32, (count, chosen.shape[1]), 0) // span
    column = lax.broadcasted_iota(jnp.int32, (count, chosen.shape[1]), 1)
    for w in (0, 1):
        hit = jnp.where(column == query + (x ^ w) * (count // span), 1.0, 0.0)
        chosen[w * count : (w + 1) * count, :] = hit.astype(chosen.dtype)


def finish(act, tile, width):
    rows = act.shape[0] // 2
    gate_act, up_act = act[:rows], act[rows:]
    hidden = (gate_act / (1.0 + jnp.exp(-gate_act)) * up_act).astype(jnp.bfloat16)
    folded = jnp.concatenate([tile[:, i * width : (i + 1) * width] for i in range(rows // FOLD)], axis=0)
    return dot(folded, hidden, TN)


def through(x, cores, width):
    total = None
    for blocks, fold in cores:
        part = finish(dot(jnp.concatenate(blocks, axis=0), x, NT), fold, width)
        total = part if total is None else total + part
    return total


def own_cores(gate, up, fold, pair_gate, pair_up, pair_fold):
    return [([gate[...], up[...]], fold[...]), ([pair_gate[...], pair_up[...]], pair_fold[...])]


def other_cores(*refs):
    first = lax.axis_index(G) == 0
    cores = []
    for mine, others, rest_gate, rest_up in (refs[:4], refs[4:]):
        left = rest_up.shape[0]
        gate, up = jnp.where(first, mine[...], others[...]), jnp.where(first, others[...], mine[...])
        cores.append(([gate, rest_gate[:left, :], up, rest_up[...]], rest_gate[left:, :]))
    return cores


def at_end():
    z = lax.axis_index(E)
    return (z == 0) | (z == lax.axis_size(E) - 1)


def first_body(tokens, near, *refs):
    *own, got = refs
    x = jnp.concatenate([tokens[...], near[...]], axis=0)
    got[...] = through(x, own_cores(*own), got.shape[0])


def two_body(end_two, far_inner, *refs):
    *own, got = refs
    got[...] = through(jnp.where(at_end(), end_two[...], far_inner[...]), own_cores(*own), got.shape[0])


def second_body(tokens, near, end_two, far_inner, got_own, got_two, *refs):
    other, (here, back_near, back_two) = refs[:8], refs[8:]
    n, width = tokens.shape[0], got_own.shape[0]
    two = jnp.where(at_end(), end_two[...], far_inner[...])
    got = through(jnp.concatenate([tokens[...], near[...], two], axis=0), other_cores(*other), width)
    mine = [got_own[:, :n], got_own[:, n:], got_two[...]]
    for k, to in enumerate((here, back_near, back_two)):
        to[:width, :] = mine[k].astype(to.dtype)
        to[width : 2 * width, :] = got[:, k * n : (k + 1) * n].astype(to.dtype)
        if k:
            to[2 * width :, :] = jnp.zeros((to.shape[0] - 2 * width, n), to.dtype)


def third_body(end_three, across, earlier, *refs):
    own, other, to = refs[:6], refs[6:14], refs[14]
    width = to.shape[0] // 2
    three = jnp.where(at_end(), end_three[...], across[...])
    to[:width, :] = through(three, own_cores(*own), width).astype(to.dtype)
    to[width:, :] = through(three, other_cores(*other), width).astype(to.dtype)


def score_body(base, here, near, two, three, weights, live, chosen, queries, others, scores):
    width, tokens = base.shape
    total = base[...]
    for k, sent in enumerate((here, near, two, three)):
        for w in (0, 1):
            part = sent[w * width : (w + 1) * width, :].astype(jnp.float32)
            total = total + weights[2 * k + w : 2 * k + w + 1, :] * part
    norm = jnp.sqrt(jnp.sum(total * total, axis=0, keepdims=True) + 1e-06)
    embedding = (total / norm).T.astype(jnp.bfloat16)
    best = [[] for _ in range(tokens // PLEN)]
    for block in (queries, others):
        raw = dot(embedding, block[...], NT) + live[:, :1]
        for p, found in enumerate(best):
            found.append(jnp.max(raw[p * PLEN : (p + 1) * PLEN], axis=0, keepdims=True))
    left = jnp.concatenate([jnp.concatenate(found, axis=1) for found in best], axis=0)
    thirds = []
    for _ in range(3):
        thirds.append(left.astype(jnp.bfloat16))
        left = left - thirds[-1].astype(jnp.float32)
    sums = [dot(third, chosen[...]) for third in thirds]
    scores[...] = sums[0] + (sums[1] + sums[2])


def by_column(
    tokens, route_ids, gate_values, passage_lengths, gate_weight, up_weight, down_weight, proj_weight, queries
):
    n, model_width = tokens.shape
    hidden_part = gate_weight.shape[2]
    width = proj_weight.shape[1]
    swap = [(0, 1), (1, 0)]
    ends, middle = [(1, 0), (2, 3)], [(1, 2), (2, 1)]
    f32, bf16 = jnp.float32, jnp.bfloat16

    rows = queries.shape[0] * queries.shape[1]
    both, longer = (2 * width, n), (2 * width + FOLD, n)
    near = lax.ppermute(tokens, E, [(i, i ^ 1) for i in range(4)])
    across = lax.ppermute(tokens, E, middle)
    gate, up, down = gate_weight[0].T, up_weight[0].T, down_weight[0].T
    part_rows = min(2 * hidden_part // 3, n - 1) // 16 * 16
    left = hidden_part - part_rows
    (part,) = kernel(part_body, [gate, up], [((part_rows, model_width), bf16)])
    part_x = lax.ppermute(part, Q, swap)
    fold, rest_gate, rest_up, held_gate, held_up, base, weights, live, chosen = kernel(
        fold_body,
        [passage_lengths, tokens, gate, up, down, proj_weight, route_ids.T, gate_values.T],
        [((r, model_width), bf16) for r in (FOLD, left + FOLD, left, hidden_part, hidden_part)]
        + [((width, n), f32), ((8, n), f32), ((n, width), f32), ((2 * rows, 2 * queries.shape[0]), bf16)],
        smem=(0,),
        fetched=(1,),
    )
    pair_gate, pair_up = lax.ppermute(gate, D, swap), lax.ppermute(up, D, swap)
    pair_fold = lax.ppermute(tied([fold], [pair_gate], 1)[0], D, swap)
    own = [held_gate, held_up, fold, pair_gate, pair_up, pair_fold]
    (got_own,) = kernel(first_body, [tokens, near, *own], [((width, 2 * n), f32)], fetched=(0,))

    far_inner = lax.ppermute(near, E, middle)
    end_two = lax.ppermute(across, E, ends)
    rest_x = [lax.ppermute(a, Q, swap) for a in (*tied([rest_gate], [pair_gate, pair_up], 1), *tied([rest_up], [near, across], 1))]
    (part_x,) = tied([part_x], [near, across], 1)
    part_y = lax.ppermute(part_x, G, swap)
    (got_two,) = kernel(two_body, [end_two, far_inner, *own], [((width, n), f32)])

    end_three = lax.ppermute(far_inner, E, ends)
    other = [part_x, part_y, *rest_x]
    free = {i: lax.ppermute(other[i], D, swap) for i in (2,)}
    held = dict(zip((0, 1, 3), tied([other[i] for i in (0, 1, 3)], [far_inner, got_own, got_two, free[2]], 1)))
    other = other + [free[i] if i in free else lax.ppermute(held[i], D, swap) for i in range(4)]
    other_queries = lax.ppermute(queries, Q, swap)
    here, *back = kernel(
        second_body,
        [tokens, near, end_two, far_inner, got_own, got_two, *other],
        [(both, f32), (longer, bf16), (longer, bf16)],
        fetched=(0,),
    )
    back += kernel(third_body, [end_three, across, here, *own, *other], [(both, bf16)])
    from_near, two, three = (
        lax.ppermute(a, E, [(i, i ^ k) for i in range(4)]) for k, a in enumerate(back, start=1)
    )
    (scores,) = kernel(
        score_body,
        [
            base, here, from_near, two, three, weights, live, chosen,
            queries.reshape(rows, width), other_queries.reshape(rows, width),
        ],
        [((n // PLEN, 2 * queries.shape[0]), f32)],
    )
    return scores


def solution(mesh):
    in_specs = (
        P((G, E, Q, D), None),
        P((G, E, Q, D), None),
        P((G, E, Q, D), None),
        P((G, E, Q, D)),
        P((E, Q), None, D),
        P((E, Q), None, D),
        P((E, Q), None, D),
        P(),
        P((G, Q), None, None),
    )
    sizes = [mesh.shape[a] for a in (G, E, Q, D)]
    return jax.shard_map(
        by_column if sizes == [2, 4, 2, 2] else by_dispatch,
        mesh=mesh,
        in_specs=in_specs,
        out_specs=P((G, E, Q, D), None),
        check_vma=False,
    )
```

```python
import jax
import jax.numpy as jnp
from jax import lax
from jax.experimental import pallas as pl
from jax.experimental.pallas import tpu as pltpu
from jax.sharding import PartitionSpec as P

PLEN = 64
G, E, Q, D = "group", "expert", "query", "dp"


def matched(embedding, live_mask, block_queries):
    query_rows = block_queries.reshape(-1, block_queries.shape[-1])
    raw_scores = jnp.dot(embedding, query_rows.T, preferred_element_type=jnp.float32)
    raw_scores = jnp.where(live_mask[:, None], raw_scores, -jnp.inf)
    best_match = jnp.max(raw_scores.reshape(-1, PLEN, raw_scores.shape[-1]), axis=1)
    return jnp.sum(best_match.reshape(best_match.shape[0], -1, block_queries.shape[1]), axis=-1)


def embedded(projected):
    lengths_norm = jnp.sqrt(jnp.sum(projected * projected, axis=-1, keepdims=True) + 1e-06)
    return (projected / lengths_norm).astype(jnp.bfloat16)


def live_tokens(passage_lengths, tok_rows):
    position = jnp.arange(tok_rows, dtype=jnp.int32) % PLEN
    return position < jnp.repeat(passage_lengths, PLEN)


def by_dispatch(
    tokens, route_ids, gate_values, passage_lengths, gate_weight, up_weight, down_weight, proj_weight, queries
):
    tok_rows, model_width = tokens.shape
    top_count = route_ids.shape[1]
    experts = lax.axis_size(E) * lax.axis_size(Q)
    capacity = max(2, 2 * tok_rows * top_count // experts)
    assignments = tok_rows * top_count
    flat_routes = route_ids.reshape(-1)
    one_hot = flat_routes[:, None] == jnp.arange(experts, dtype=jnp.int32)[None, :]
    order = jnp.arange(assignments, dtype=jnp.int32)
    before = (order[None, :] < order[:, None]).astype(jnp.bfloat16)
    earlier = jnp.dot(before, one_hot.astype(jnp.bfloat16), preferred_element_type=jnp.float32)
    slot_index = jnp.sum(jnp.where(one_hot, earlier, 0.0), axis=1).astype(jnp.int32)
    slot_target = flat_routes * capacity + slot_index
    slot_owner = jnp.full((experts * capacity,), assignments, jnp.int32).at[slot_target].set(order)
    padded = jnp.concatenate([tokens, jnp.zeros((1, model_width), tokens.dtype)], axis=0)
    source_row = jnp.where(slot_owner < assignments, slot_owner // top_count, tok_rows)
    outgoing = padded[source_row].reshape(experts, capacity, model_width)
    arrived = lax.all_to_all(outgoing, (E, Q), split_axis=0, concat_axis=0, tiled=True)
    expert_rows = arrived.reshape(experts * capacity, model_width)
    gate_act = jnp.dot(
        expert_rows, lax.all_gather(gate_weight[0], D, axis=1, tiled=True), preferred_element_type=jnp.float32
    )
    up_act = jnp.dot(
        expert_rows, lax.all_gather(up_weight[0], D, axis=1, tiled=True), preferred_element_type=jnp.float32
    )
    hidden = (jax.nn.silu(gate_act) * up_act).astype(jnp.bfloat16)
    results = lax.dot_general(
        hidden,
        lax.all_gather(down_weight[0], D, axis=1, tiled=True),
        (((1,), (1,)), ((), ())),
        preferred_element_type=jnp.float32,
    ).astype(jnp.bfloat16)
    folded = jnp.dot(results, proj_weight, preferred_element_type=jnp.float32)
    returned_rows = lax.all_to_all(
        folded.reshape(experts, capacity, folded.shape[-1]), (E, Q), split_axis=0, concat_axis=0, tiled=True
    )
    picked = returned_rows.reshape(experts * capacity, folded.shape[-1])[slot_target]
    weights = gate_values.reshape(assignments, 1)
    projected = jnp.dot(tokens, proj_weight, preferred_element_type=jnp.float32) + jnp.sum(
        (picked * weights).reshape(tok_rows, top_count, folded.shape[-1]), axis=1
    )
    live_mask = live_tokens(passage_lengths, tok_rows)
    return matched(embedded(projected), live_mask, lax.all_gather(queries, Q, axis=0, tiled=True))


VMEM = pl.BlockSpec(memory_space=pltpu.VMEM)
SMEM = pl.BlockSpec(memory_space=pltpu.SMEM)
NT, TN = (((1,), (1,)), ((), ())), (((0,), (0,)), ((), ()))


def dot(a, b, dims=(((1,), (0,)), ((), ()))):
    return lax.dot_general(a, b, dims, preferred_element_type=jnp.float32)


def whole_block(a):
    return pl.BlockSpec(a.shape, lambda *_: (0,) * a.ndim)


def tied(values, after, parts):
    def body(*refs):
        outs = refs[len(values) + len(after) :]
        for i in range(len(values)):
            rows = outs[parts * i].shape[0]
            for p in range(parts):
                outs[parts * i + p][...] = refs[i][p * rows : (p + 1) * rows, :]

    blocks = [jax.ShapeDtypeStruct((a.shape[0] // parts, a.shape[1]), a.dtype) for a in values for _ in range(parts)]

    return pl.pallas_call(
        body,
        out_shape=blocks,
        in_specs=[VMEM] * len(values) + [pl.BlockSpec(memory_space=pl.ANY)] * len(after),
        out_specs=[VMEM] * len(blocks),
        compiler_params=pltpu.CompilerParams(vmem_limit_bytes=8 * 2**20),
    )(*values, *after)


def kernel(body, operands, outs, smem=(), fetched=(), limit=24, flops=0):
    return pl.pallas_call(
        body,
        out_shape=[jax.ShapeDtypeStruct(shape, dtype) for shape, dtype in outs],
        in_specs=[
            SMEM if i in smem else whole_block(a) if i in fetched else VMEM for i, a in enumerate(operands)
        ],
        out_specs=[VMEM] * len(outs),
        compiler_params=pltpu.CompilerParams(vmem_limit_bytes=limit * 2**20),
        cost_estimate=pl.CostEstimate(flops=flops, bytes_accessed=0, transcendentals=0),
    )(*operands)


FOLD = 16


def part_body(gate, up, part):
    rows = part.shape[0]
    part[...] = jnp.where(lax.axis_index(G) == 0, gate[:rows, :], up[:rows, :])


def fold_body(
    lengths, tokens, gate, up, down, proj, routes, gates,
    fold, rest_gate, rest_up, held_gate, held_up, base, weights, live, chosen,
):
    rows, width = down.shape[0], proj.shape[1]
    folded = dot(down[...], proj[...]).astype(jnp.bfloat16)
    fold[...] = jnp.zeros_like(fold)
    for i in range(rows // FOLD):
        fold[:, i * width : (i + 1) * width] = folded[i * FOLD : (i + 1) * FOLD]
    left = rest_gate.shape[0]
    rest_gate[...] = gate[rows - left :, :]
    rest_up[:left, :] = up[rows - left :, :]
    rest_up[left:, :] = fold[...]
    held_gate[...] = gate[...]
    held_up[...] = up[...]
    base[...] = dot(tokens[...], proj[...]).T
    z, x = lax.axis_index(E), lax.axis_index(Q)
    for i in range(weights.shape[0]):
        expert = (z ^ (i // 2)) * 2 + (x ^ (i % 2))
        weights[i : i + 1, :] = jnp.sum(jnp.where(routes[...] == expert, gates[...], 0.0), axis=0, keepdims=True)
    position = lax.broadcasted_iota(jnp.int32, (PLEN, live.shape[1]), 0)
    for p in range(live.shape[0] // PLEN):
        live[p * PLEN : (p + 1) * PLEN, :] = jnp.where(position < lengths[p], 0.0, -jnp.inf)
    count, span = chosen.shape[0] // 2, chosen.shape[0] // chosen.shape[1]
    query = lax.broadcasted_iota(jnp.int32, (count, chosen.shape[1]), 0) // span
    column = lax.broadcasted_iota(jnp.int32, (count, chosen.shape[1]), 1)
    for w in (0, 1):
        hit = jnp.where(column == query + (x ^ w) * (count // span), 1.0, 0.0)
        chosen[w * count : (w + 1) * count, :] = hit.astype(chosen.dtype)


def finish(act, tile, width):
    rows = act.shape[0] // 2
    gate_act, up_act = act[:rows], act[rows:]
    hidden = (gate_act / (1.0 + jnp.exp(-gate_act)) * up_act).astype(jnp.bfloat16)
    folded = jnp.concatenate([tile[:, i * width : (i + 1) * width] for i in range(rows // FOLD)], axis=0)
    return dot(folded, hidden, TN)


def through(x, cores, width):
    total = None
    for blocks, fold in cores:
        part = finish(dot(jnp.concatenate(blocks, axis=0), x, NT), fold, width)
        total = part if total is None else total + part
    return total


def own_cores(gate, up, fold, pair_gate, pair_up, pair_fold):
    return [([gate[...], up[...]], fold[...]), ([pair_gate[...], pair_up[...]], pair_fold[...])]


def other_cores(*refs):
    first = lax.axis_index(G) == 0
    cores = []
    for mine, others, rest_gate, rest_up in (refs[:4], refs[4:]):
        left = rest_gate.shape[0]
        gate, up = jnp.where(first, mine[...], others[...]), jnp.where(first, others[...], mine[...])
        cores.append(([gate, rest_gate[...], up, rest_up[:left, :]], rest_up[left:, :]))
    return cores


def at_end():
    z = lax.axis_index(E)
    return (z == 0) | (z == lax.axis_size(E) - 1)


def first_body(tokens, near, *refs):
    *own, got = refs
    x = jnp.concatenate([tokens[...], near[...]], axis=0)
    got[...] = through(x, own_cores(*own), got.shape[0])


def two_body(end_two, far_inner, *refs):
    *own, got = refs
    got[...] = through(jnp.where(at_end(), end_two[...], far_inner[...]), own_cores(*own), got.shape[0])


def second_body(tokens, near, end_two, far_inner, got_own, got_two, *refs):
    other, (here, back_near, back_two) = refs[:8], refs[8:]
    n, width = tokens.shape[0], got_own.shape[0]
    two = jnp.where(at_end(), end_two[...], far_inner[...])
    got = through(jnp.concatenate([tokens[...], near[...], two], axis=0), other_cores(*other), width)
    mine = [got_own[:, :n], got_own[:, n:], got_two[...]]
    for k, to in enumerate((here, back_near, back_two)):
        to[:width, :] = mine[k].astype(to.dtype)
        to[width : 2 * width, :] = got[:, k * n : (k + 1) * n].astype(to.dtype)
        if k:
            to[2 * width :, :] = jnp.zeros((to.shape[0] - 2 * width, n), to.dtype)


def third_body(end_three, across, earlier, *refs):
    own, other, to = refs[:6], refs[6:14], refs[14]
    width = to.shape[0] // 2
    three = jnp.where(at_end(), end_three[...], across[...])
    to[:width, :] = through(three, own_cores(*own), width).astype(to.dtype)
    to[width:, :] = through(three, other_cores(*other), width).astype(to.dtype)


def score_body(base, here, near, two, three, weights, live, chosen, queries, others, scores):
    width, tokens = base.shape
    total = base[...]
    for k, sent in enumerate((here, near, two, three)):
        for w in (0, 1):
            part = sent[w * width : (w + 1) * width, :].astype(jnp.float32)
            total = total + weights[2 * k + w : 2 * k + w + 1, :] * part
    norm = jnp.sqrt(jnp.sum(total * total, axis=0, keepdims=True) + 1e-06)
    embedding = (total / norm).T.astype(jnp.bfloat16)
    best = [[] for _ in range(tokens // PLEN)]
    for block in (queries, others):
        raw = dot(embedding, block[...], NT) + live[:, :1]
        for p, found in enumerate(best):
            found.append(jnp.max(raw[p * PLEN : (p + 1) * PLEN], axis=0, keepdims=True))
    left = jnp.concatenate([jnp.concatenate(found, axis=1) for found in best], axis=0)
    thirds = []
    for _ in range(3):
        thirds.append(left.astype(jnp.bfloat16))
        left = left - thirds[-1].astype(jnp.float32)
    sums = [dot(third, chosen[...]) for third in thirds]
    scores[...] = sums[0] + (sums[1] + sums[2])


def by_column(
    tokens, route_ids, gate_values, passage_lengths, gate_weight, up_weight, down_weight, proj_weight, queries
):
    n, model_width = tokens.shape
    hidden_part = gate_weight.shape[2]
    width = proj_weight.shape[1]
    swap = [(0, 1), (1, 0)]
    ends, middle = [(1, 0), (2, 3)], [(1, 2), (2, 1)]
    f32, bf16 = jnp.float32, jnp.bfloat16

    rows = queries.shape[0] * queries.shape[1]
    both, longer = (2 * width, n), (2 * width + FOLD, n)
    near = lax.ppermute(tokens, E, [(i, i ^ 1) for i in range(4)])
    across = lax.ppermute(tokens, E, middle)
    gate, up, down = gate_weight[0].T, up_weight[0].T, down_weight[0].T
    part_rows = min(2 * hidden_part // 3, n - 1) // 16 * 16
    left = hidden_part - part_rows
    (part,) = kernel(part_body, [gate, up], [((part_rows, model_width), bf16)])
    part_x = lax.ppermute(part, Q, swap)
    fold, rest_gate, rest_up, held_gate, held_up, base, weights, live, chosen = kernel(
        fold_body,
        [passage_lengths, tokens, gate, up, down, proj_weight, route_ids.T, gate_values.T],
        [((r, model_width), bf16) for r in (FOLD, left, left + FOLD, hidden_part, hidden_part)]
        + [((width, n), f32), ((8, n), f32), ((n, width), f32), ((2 * rows, 2 * queries.shape[0]), bf16)],
        smem=(0,),
        fetched=(1,),
    )
    pair_gate, pair_up = lax.ppermute(gate, D, swap), lax.ppermute(up, D, swap)
    pair_fold = lax.ppermute(tied([fold], [pair_gate], 1)[0], D, swap)
    own = [held_gate, held_up, fold, pair_gate, pair_up, pair_fold]
    (got_own,) = kernel(first_body, [tokens, near, *own], [((width, 2 * n), f32)], fetched=(0,))

    far_inner = lax.ppermute(near, E, middle)
    end_two = lax.ppermute(across, E, ends)
    rest_x = [lax.ppermute(a, Q, swap) for a in (*tied([rest_gate], [pair_gate, pair_up], 1), *tied([rest_up], [near, across], 1))]
    (part_x,) = tied([part_x], [near, across], 1)
    part_y = lax.ppermute(part_x, G, swap)
    (got_two,) = kernel(two_body, [end_two, far_inner, *own], [((width, n), f32)])

    end_three = lax.ppermute(far_inner, E, ends)
    other = [part_x, part_y, *rest_x]
    free = {i: lax.ppermute(other[i], D, swap) for i in (2,)}
    held = dict(zip((0, 1, 3), tied([other[i] for i in (0, 1, 3)], [far_inner, got_own, got_two, free[2]], 1)))
    other = other + [free[i] if i in free else lax.ppermute(held[i], D, swap) for i in range(4)]
    other_queries = lax.ppermute(queries, Q, swap)
    here, *back = kernel(
        second_body,
        [tokens, near, end_two, far_inner, got_own, got_two, *other],
        [(both, f32), (longer, bf16), (longer, bf16)],
        fetched=(0,),
    )
    back += kernel(third_body, [end_three, across, here, *own, *other], [(both, bf16)])
    from_near, two, three = (
        lax.ppermute(a, E, [(i, i ^ k) for i in range(4)]) for k, a in enumerate(back, start=1)
    )
    (scores,) = kernel(
        score_body,
        [
            base, here, from_near, two, three, weights, live, chosen,
            queries.reshape(rows, width), other_queries.reshape(rows, width),
        ],
        [((n // PLEN, 2 * queries.shape[0]), f32)],
    )
    return scores


def solution(mesh):
    in_specs = (
        P((G, E, Q, D), None),
        P((G, E, Q, D), None),
        P((G, E, Q, D), None),
        P((G, E, Q, D)),
        P((E, Q), None, D),
        P((E, Q), None, D),
        P((E, Q), None, D),
        P(),
        P((G, Q), None, None),
    )
    sizes = [mesh.shape[a] for a in (G, E, Q, D)]
    return jax.shard_map(
        by_column if sizes == [2, 4, 2, 2] else by_dispatch,
        mesh=mesh,
        in_specs=in_specs,
        out_specs=P((G, E, Q, D), None),
        check_vma=False,
    )
```

```python
import jax
import jax.numpy as jnp
from jax import lax
from jax.experimental import pallas as pl
from jax.experimental.pallas import tpu as pltpu
from jax.sharding import PartitionSpec as P

PLEN = 64
G, E, Q, D = "group", "expert", "query", "dp"


def matched(embedding, live_mask, block_queries):
    query_rows = block_queries.reshape(-1, block_queries.shape[-1])
    raw_scores = jnp.dot(embedding, query_rows.T, preferred_element_type=jnp.float32)
    raw_scores = jnp.where(live_mask[:, None], raw_scores, -jnp.inf)
    best_match = jnp.max(raw_scores.reshape(-1, PLEN, raw_scores.shape[-1]), axis=1)
    return jnp.sum(best_match.reshape(best_match.shape[0], -1, block_queries.shape[1]), axis=-1)


def embedded(projected):
    lengths_norm = jnp.sqrt(jnp.sum(projected * projected, axis=-1, keepdims=True) + 1e-06)
    return (projected / lengths_norm).astype(jnp.bfloat16)


def live_tokens(passage_lengths, tok_rows):
    position = jnp.arange(tok_rows, dtype=jnp.int32) % PLEN
    return position < jnp.repeat(passage_lengths, PLEN)


def by_dispatch(
    tokens, route_ids, gate_values, passage_lengths, gate_weight, up_weight, down_weight, proj_weight, queries
):
    tok_rows, model_width = tokens.shape
    top_count = route_ids.shape[1]
    experts = lax.axis_size(E) * lax.axis_size(Q)
    capacity = max(2, 2 * tok_rows * top_count // experts)
    assignments = tok_rows * top_count
    flat_routes = route_ids.reshape(-1)
    one_hot = flat_routes[:, None] == jnp.arange(experts, dtype=jnp.int32)[None, :]
    order = jnp.arange(assignments, dtype=jnp.int32)
    before = (order[None, :] < order[:, None]).astype(jnp.bfloat16)
    earlier = jnp.dot(before, one_hot.astype(jnp.bfloat16), preferred_element_type=jnp.float32)
    slot_index = jnp.sum(jnp.where(one_hot, earlier, 0.0), axis=1).astype(jnp.int32)
    slot_target = flat_routes * capacity + slot_index
    slot_owner = jnp.full((experts * capacity,), assignments, jnp.int32).at[slot_target].set(order)
    padded = jnp.concatenate([tokens, jnp.zeros((1, model_width), tokens.dtype)], axis=0)
    source_row = jnp.where(slot_owner < assignments, slot_owner // top_count, tok_rows)
    outgoing = padded[source_row].reshape(experts, capacity, model_width)
    arrived = lax.all_to_all(outgoing, (E, Q), split_axis=0, concat_axis=0, tiled=True)
    expert_rows = arrived.reshape(experts * capacity, model_width)
    gate_act = jnp.dot(
        expert_rows, lax.all_gather(gate_weight[0], D, axis=1, tiled=True), preferred_element_type=jnp.float32
    )
    up_act = jnp.dot(
        expert_rows, lax.all_gather(up_weight[0], D, axis=1, tiled=True), preferred_element_type=jnp.float32
    )
    hidden = (jax.nn.silu(gate_act) * up_act).astype(jnp.bfloat16)
    results = lax.dot_general(
        hidden,
        lax.all_gather(down_weight[0], D, axis=1, tiled=True),
        (((1,), (1,)), ((), ())),
        preferred_element_type=jnp.float32,
    ).astype(jnp.bfloat16)
    folded = jnp.dot(results, proj_weight, preferred_element_type=jnp.float32)
    returned_rows = lax.all_to_all(
        folded.reshape(experts, capacity, folded.shape[-1]), (E, Q), split_axis=0, concat_axis=0, tiled=True
    )
    picked = returned_rows.reshape(experts * capacity, folded.shape[-1])[slot_target]
    weights = gate_values.reshape(assignments, 1)
    projected = jnp.dot(tokens, proj_weight, preferred_element_type=jnp.float32) + jnp.sum(
        (picked * weights).reshape(tok_rows, top_count, folded.shape[-1]), axis=1
    )
    live_mask = live_tokens(passage_lengths, tok_rows)
    return matched(embedded(projected), live_mask, lax.all_gather(queries, Q, axis=0, tiled=True))


VMEM = pl.BlockSpec(memory_space=pltpu.VMEM)
SMEM = pl.BlockSpec(memory_space=pltpu.SMEM)
NT, TN = (((1,), (1,)), ((), ())), (((0,), (0,)), ((), ()))


def dot(a, b, dims=(((1,), (0,)), ((), ()))):
    return lax.dot_general(a, b, dims, preferred_element_type=jnp.float32)


def whole_block(a):
    return pl.BlockSpec(a.shape, lambda *_: (0,) * a.ndim)


def tied(values, after, parts):
    def body(*refs):
        outs = refs[len(values) + len(after) :]
        for i in range(len(values)):
            rows = outs[parts * i].shape[0]
            for p in range(parts):
                outs[parts * i + p][...] = refs[i][p * rows : (p + 1) * rows, :]

    blocks = [jax.ShapeDtypeStruct((a.shape[0] // parts, a.shape[1]), a.dtype) for a in values for _ in range(parts)]

    return pl.pallas_call(
        body,
        out_shape=blocks,
        in_specs=[VMEM] * len(values) + [pl.BlockSpec(memory_space=pl.ANY)] * len(after),
        out_specs=[VMEM] * len(blocks),
        compiler_params=pltpu.CompilerParams(vmem_limit_bytes=8 * 2**20),
    )(*values, *after)


def kernel(body, operands, outs, smem=(), fetched=(), limit=24, flops=0):
    return pl.pallas_call(
        body,
        out_shape=[jax.ShapeDtypeStruct(shape, dtype) for shape, dtype in outs],
        in_specs=[
            SMEM if i in smem else whole_block(a) if i in fetched else VMEM for i, a in enumerate(operands)
        ],
        out_specs=[VMEM] * len(outs),
        compiler_params=pltpu.CompilerParams(vmem_limit_bytes=limit * 2**20),
        cost_estimate=pl.CostEstimate(flops=flops, bytes_accessed=0, transcendentals=0),
    )(*operands)


FOLD = 16


def part_body(gate, up, part):
    rows = part.shape[0]
    part[...] = jnp.where(lax.axis_index(G) == 0, gate[:rows, :], up[:rows, :])


def fold_body(
    lengths, tokens, gate, up, down, proj, routes, gates,
    fold, rest_gate, rest_up, held_gate, held_up, base, weights, live, chosen,
):
    rows, width = down.shape[0], proj.shape[1]
    folded = dot(down[...], proj[...]).astype(jnp.bfloat16)
    fold[...] = jnp.zeros_like(fold)
    for i in range(rows // FOLD):
        fold[:, i * width : (i + 1) * width] = folded[i * FOLD : (i + 1) * FOLD]
    left = rest_gate.shape[0]
    rest_gate[...] = gate[rows - left :, :]
    rest_up[:left, :] = up[rows - left :, :]
    rest_up[left:, :] = fold[...]
    held_gate[...] = gate[...]
    held_up[...] = up[...]
    base[...] = dot(tokens[...], proj[...]).T
    z, x = lax.axis_index(E), lax.axis_index(Q)
    for i in range(weights.shape[0]):
        expert = (z ^ (i // 2)) * 2 + (x ^ (i % 2))
        weights[i : i + 1, :] = jnp.sum(jnp.where(routes[...] == expert, gates[...], 0.0), axis=0, keepdims=True)
    position = lax.broadcasted_iota(jnp.int32, (PLEN, live.shape[1]), 0)
    for p in range(live.shape[0] // PLEN):
        live[p * PLEN : (p + 1) * PLEN, :] = jnp.where(position < lengths[p], 0.0, -jnp.inf)
    count, span = chosen.shape[0] // 2, chosen.shape[0] // chosen.shape[1]
    query = lax.broadcasted_iota(jnp.int32, (count, chosen.shape[1]), 0) // span
    column = lax.broadcasted_iota(jnp.int32, (count, chosen.shape[1]), 1)
    for w in (0, 1):
        hit = jnp.where(column == query + (x ^ w) * (count // span), 1.0, 0.0)
        chosen[w * count : (w + 1) * count, :] = hit.astype(chosen.dtype)


def finish(act, tile, width):
    rows = act.shape[0] // 2
    gate_act, up_act = act[:rows], act[rows:]
    hidden = (gate_act / (1.0 + jnp.exp(-gate_act)) * up_act).astype(jnp.bfloat16)
    folded = jnp.concatenate([tile[:, i * width : (i + 1) * width] for i in range(rows // FOLD)], axis=0)
    return dot(folded, hidden, TN)


def through(x, cores, width):
    total = None
    for blocks, fold in cores:
        part = finish(dot(jnp.concatenate(blocks, axis=0), x, NT), fold, width)
        total = part if total is None else total + part
    return total


def own_cores(gate, up, fold, pair_gate, pair_up, pair_fold):
    return [([gate[...], up[...]], fold[...]), ([pair_gate[...], pair_up[...]], pair_fold[...])]


def other_cores(*refs):
    first = lax.axis_index(G) == 0
    cores = []
    for mine, others, rest_gate, rest_up in (refs[:4], refs[4:]):
        left = rest_gate.shape[0]
        gate, up = jnp.where(first, mine[...], others[...]), jnp.where(first, others[...], mine[...])
        cores.append(([gate, rest_gate[...], up, rest_up[:left, :]], rest_up[left:, :]))
    return cores


def at_end():
    z = lax.axis_index(E)
    return (z == 0) | (z == lax.axis_size(E) - 1)


def first_body(tokens, near, *refs):
    *own, got = refs
    x = jnp.concatenate([tokens[...], near[...]], axis=0)
    got[...] = through(x, own_cores(*own), got.shape[0])


def two_body(end_two, far_inner, *refs):
    *own, got = refs
    got[...] = through(jnp.where(at_end(), end_two[...], far_inner[...]), own_cores(*own), got.shape[0])


def second_body(tokens, near, end_two, far_inner, got_own, got_two, *refs):
    other, (here, back_near, back_two) = refs[:8], refs[8:]
    n, width = tokens.shape[0], got_own.shape[0]
    two = jnp.where(at_end(), end_two[...], far_inner[...])
    got = through(jnp.concatenate([tokens[...], near[...], two], axis=0), other_cores(*other), width)
    mine = [got_own[:, :n], got_own[:, n:], got_two[...]]
    for k, to in enumerate((here, back_near, back_two)):
        to[:width, :] = mine[k].astype(to.dtype)
        to[width : 2 * width, :] = got[:, k * n : (k + 1) * n].astype(to.dtype)
        if k:
            to[2 * width :, :] = jnp.zeros((to.shape[0] - 2 * width, n), to.dtype)


def third_body(end_three, across, earlier, *refs):
    own, other, to = refs[:6], refs[6:14], refs[14]
    width = to.shape[0] // 2
    three = jnp.where(at_end(), end_three[...], across[...])
    to[:width, :] = through(three, own_cores(*own), width).astype(to.dtype)
    to[width:, :] = through(three, other_cores(*other), width).astype(to.dtype)


def score_body(base, here, near, two, three, weights, live, chosen, queries, others, scores):
    width, tokens = base.shape
    total = base[...]
    for k, sent in enumerate((here, near, two, three)):
        for w in (0, 1):
            part = sent[w * width : (w + 1) * width, :].astype(jnp.float32)
            total = total + weights[2 * k + w : 2 * k + w + 1, :] * part
    norm = jnp.sqrt(jnp.sum(total * total, axis=0, keepdims=True) + 1e-06)
    embedding = (total / norm).T.astype(jnp.bfloat16)
    best = [[] for _ in range(tokens // PLEN)]
    for block in (queries, others):
        raw = dot(embedding, block[...], NT) + live[:, :1]
        for p, found in enumerate(best):
            found.append(jnp.max(raw[p * PLEN : (p + 1) * PLEN], axis=0, keepdims=True))
    left = jnp.concatenate([jnp.concatenate(found, axis=1) for found in best], axis=0)
    thirds = []
    for _ in range(3):
        thirds.append(left.astype(jnp.bfloat16))
        left = left - thirds[-1].astype(jnp.float32)
    sums = [dot(third, chosen[...]) for third in thirds]
    scores[...] = sums[0] + (sums[1] + sums[2])


def by_column(
    tokens, route_ids, gate_values, passage_lengths, gate_weight, up_weight, down_weight, proj_weight, queries
):
    n, model_width = tokens.shape
    hidden_part = gate_weight.shape[2]
    width = proj_weight.shape[1]
    swap = [(0, 1), (1, 0)]
    ends, middle = [(1, 0), (2, 3)], [(1, 2), (2, 1)]
    f32, bf16 = jnp.float32, jnp.bfloat16

    rows = queries.shape[0] * queries.shape[1]
    both, longer = (2 * width, n), (2 * width + FOLD, n)
    near = lax.ppermute(tokens, E, [(i, i ^ 1) for i in range(4)])
    across = lax.ppermute(tokens, E, middle)
    gate, up, down = gate_weight[0].T, up_weight[0].T, down_weight[0].T
    part_rows = hidden_part // 2 // 16 * 16
    left = hidden_part - part_rows
    (part,) = kernel(part_body, [gate, up], [((part_rows, model_width), bf16)])
    part_x = lax.ppermute(part, Q, swap)
    fold, rest_gate, rest_up, held_gate, held_up, base, weights, live, chosen = kernel(
        fold_body,
        [passage_lengths, tokens, gate, up, down, proj_weight, route_ids.T, gate_values.T],
        [((r, model_width), bf16) for r in (FOLD, left, left + FOLD, hidden_part, hidden_part)]
        + [((width, n), f32), ((8, n), f32), ((n, width), f32), ((2 * rows, 2 * queries.shape[0]), bf16)],
        smem=(0,),
        fetched=(1,),
    )
    pair_gate, pair_up = lax.ppermute(gate, D, swap), lax.ppermute(up, D, swap)
    pair_fold = lax.ppermute(tied([fold], [pair_gate], 1)[0], D, swap)
    own = [held_gate, held_up, fold, pair_gate, pair_up, pair_fold]
    (got_own,) = kernel(first_body, [tokens, near, *own], [((width, 2 * n), f32)], fetched=(0,))

    far_inner = lax.ppermute(near, E, middle)
    end_two = lax.ppermute(across, E, ends)
    rest_x = [lax.ppermute(a, Q, swap) for a in (*tied([rest_gate], [pair_gate, pair_up], 1), *tied([rest_up], [near, across], 1))]
    (part_x,) = tied([part_x], [near, across], 1)
    part_y = lax.ppermute(part_x, G, swap)
    (got_two,) = kernel(two_body, [end_two, far_inner, *own], [((width, n), f32)])

    end_three = lax.ppermute(far_inner, E, ends)
    other = [part_x, part_y, *rest_x]
    free = {i: lax.ppermute(other[i], D, swap) for i in (2,)}
    held = dict(zip((0, 1, 3), tied([other[i] for i in (0, 1, 3)], [far_inner, got_own, got_two, free[2]], 1)))
    other = other + [free[i] if i in free else lax.ppermute(held[i], D, swap) for i in range(4)]
    other_queries = lax.ppermute(queries, Q, swap)
    here, *back = kernel(
        second_body,
        [tokens, near, end_two, far_inner, got_own, got_two, *other],
        [(both, f32), (longer, bf16), (longer, bf16)],
        fetched=(0,),
    )
    back += kernel(third_body, [end_three, across, here, *own, *other], [(both, bf16)])
    from_near, two, three = (
        lax.ppermute(a, E, [(i, i ^ k) for i in range(4)]) for k, a in enumerate(back, start=1)
    )
    (scores,) = kernel(
        score_body,
        [
            base, here, from_near, two, three, weights, live, chosen,
            queries.reshape(rows, width), other_queries.reshape(rows, width),
        ],
        [((n // PLEN, 2 * queries.shape[0]), f32)],
    )
    return scores


def solution(mesh):
    in_specs = (
        P((G, E, Q, D), None),
        P((G, E, Q, D), None),
        P((G, E, Q, D), None),
        P((G, E, Q, D)),
        P((E, Q), None, D),
        P((E, Q), None, D),
        P((E, Q), None, D),
        P(),
        P((G, Q), None, None),
    )
    sizes = [mesh.shape[a] for a in (G, E, Q, D)]
    return jax.shard_map(
        by_column if sizes == [2, 4, 2, 2] else by_dispatch,
        mesh=mesh,
        in_specs=in_specs,
        out_specs=P((G, E, Q, D), None),
        check_vma=False,
    )
```

```python
import jax
import jax.numpy as jnp
from jax import lax
from jax.experimental import pallas as pl
from jax.experimental.pallas import tpu as pltpu
from jax.sharding import PartitionSpec as P

PLEN = 64
G, E, Q, D = "group", "expert", "query", "dp"


def matched(embedding, live_mask, block_queries):
    query_rows = block_queries.reshape(-1, block_queries.shape[-1])
    raw_scores = jnp.dot(embedding, query_rows.T, preferred_element_type=jnp.float32)
    raw_scores = jnp.where(live_mask[:, None], raw_scores, -jnp.inf)
    best_match = jnp.max(raw_scores.reshape(-1, PLEN, raw_scores.shape[-1]), axis=1)
    return jnp.sum(best_match.reshape(best_match.shape[0], -1, block_queries.shape[1]), axis=-1)


def embedded(projected):
    lengths_norm = jnp.sqrt(jnp.sum(projected * projected, axis=-1, keepdims=True) + 1e-06)
    return (projected / lengths_norm).astype(jnp.bfloat16)


def live_tokens(passage_lengths, tok_rows):
    position = jnp.arange(tok_rows, dtype=jnp.int32) % PLEN
    return position < jnp.repeat(passage_lengths, PLEN)


def by_dispatch(
    tokens, route_ids, gate_values, passage_lengths, gate_weight, up_weight, down_weight, proj_weight, queries
):
    tok_rows, model_width = tokens.shape
    top_count = route_ids.shape[1]
    experts = lax.axis_size(E) * lax.axis_size(Q)
    capacity = max(2, 2 * tok_rows * top_count // experts)
    assignments = tok_rows * top_count
    flat_routes = route_ids.reshape(-1)
    one_hot = flat_routes[:, None] == jnp.arange(experts, dtype=jnp.int32)[None, :]
    order = jnp.arange(assignments, dtype=jnp.int32)
    before = (order[None, :] < order[:, None]).astype(jnp.bfloat16)
    earlier = jnp.dot(before, one_hot.astype(jnp.bfloat16), preferred_element_type=jnp.float32)
    slot_index = jnp.sum(jnp.where(one_hot, earlier, 0.0), axis=1).astype(jnp.int32)
    slot_target = flat_routes * capacity + slot_index
    slot_owner = jnp.full((experts * capacity,), assignments, jnp.int32).at[slot_target].set(order)
    padded = jnp.concatenate([tokens, jnp.zeros((1, model_width), tokens.dtype)], axis=0)
    source_row = jnp.where(slot_owner < assignments, slot_owner // top_count, tok_rows)
    outgoing = padded[source_row].reshape(experts, capacity, model_width)
    arrived = lax.all_to_all(outgoing, (E, Q), split_axis=0, concat_axis=0, tiled=True)
    expert_rows = arrived.reshape(experts * capacity, model_width)
    gate_act = jnp.dot(
        expert_rows, lax.all_gather(gate_weight[0], D, axis=1, tiled=True), preferred_element_type=jnp.float32
    )
    up_act = jnp.dot(
        expert_rows, lax.all_gather(up_weight[0], D, axis=1, tiled=True), preferred_element_type=jnp.float32
    )
    hidden = (jax.nn.silu(gate_act) * up_act).astype(jnp.bfloat16)
    results = lax.dot_general(
        hidden,
        lax.all_gather(down_weight[0], D, axis=1, tiled=True),
        (((1,), (1,)), ((), ())),
        preferred_element_type=jnp.float32,
    ).astype(jnp.bfloat16)
    folded = jnp.dot(results, proj_weight, preferred_element_type=jnp.float32)
    returned_rows = lax.all_to_all(
        folded.reshape(experts, capacity, folded.shape[-1]), (E, Q), split_axis=0, concat_axis=0, tiled=True
    )
    picked = returned_rows.reshape(experts * capacity, folded.shape[-1])[slot_target]
    weights = gate_values.reshape(assignments, 1)
    projected = jnp.dot(tokens, proj_weight, preferred_element_type=jnp.float32) + jnp.sum(
        (picked * weights).reshape(tok_rows, top_count, folded.shape[-1]), axis=1
    )
    live_mask = live_tokens(passage_lengths, tok_rows)
    return matched(embedded(projected), live_mask, lax.all_gather(queries, Q, axis=0, tiled=True))


VMEM = pl.BlockSpec(memory_space=pltpu.VMEM)
SMEM = pl.BlockSpec(memory_space=pltpu.SMEM)
NT, TN = (((1,), (1,)), ((), ())), (((0,), (0,)), ((), ()))


def dot(a, b, dims=(((1,), (0,)), ((), ()))):
    return lax.dot_general(a, b, dims, preferred_element_type=jnp.float32)


def whole_block(a):
    return pl.BlockSpec(a.shape, lambda *_: (0,) * a.ndim)


def tied(values, after, parts):
    def body(*refs):
        outs = refs[len(values) + len(after) :]
        for i in range(len(values)):
            rows = outs[parts * i].shape[0]
            for p in range(parts):
                outs[parts * i + p][...] = refs[i][p * rows : (p + 1) * rows, :]

    blocks = [jax.ShapeDtypeStruct((a.shape[0] // parts, a.shape[1]), a.dtype) for a in values for _ in range(parts)]

    return pl.pallas_call(
        body,
        out_shape=blocks,
        in_specs=[VMEM] * len(values) + [pl.BlockSpec(memory_space=pl.ANY)] * len(after),
        out_specs=[VMEM] * len(blocks),
        compiler_params=pltpu.CompilerParams(vmem_limit_bytes=8 * 2**20),
    )(*values, *after)


def kernel(body, operands, outs, smem=(), fetched=(), limit=24, flops=0):
    return pl.pallas_call(
        body,
        out_shape=[jax.ShapeDtypeStruct(shape, dtype) for shape, dtype in outs],
        in_specs=[
            SMEM if i in smem else whole_block(a) if i in fetched else VMEM for i, a in enumerate(operands)
        ],
        out_specs=[VMEM] * len(outs),
        compiler_params=pltpu.CompilerParams(vmem_limit_bytes=limit * 2**20),
        cost_estimate=pl.CostEstimate(flops=flops, bytes_accessed=0, transcendentals=0),
    )(*operands)


FOLD = 16


def part_body(gate, up, part):
    rows = part.shape[0]
    part[...] = jnp.where(lax.axis_index(G) == 0, gate[:rows, :], up[:rows, :])


def fold_body(
    lengths, tokens, gate, up, down, proj, routes, gates,
    fold, rest_gate, rest_up, held_gate, held_up, base, weights, live, chosen,
):
    rows, width = down.shape[0], proj.shape[1]
    folded = dot(down[...], proj[...]).astype(jnp.bfloat16)
    fold[...] = jnp.zeros_like(fold)
    for i in range(rows // FOLD):
        fold[:, i * width : (i + 1) * width] = folded[i * FOLD : (i + 1) * FOLD]
    left = rest_gate.shape[0]
    rest_gate[...] = gate[rows - left :, :]
    rest_up[:left, :] = up[rows - left :, :]
    rest_up[left:, :] = fold[...]
    held_gate[...] = gate[...]
    held_up[...] = up[...]
    base[...] = dot(tokens[...], proj[...]).T
    z, x = lax.axis_index(E), lax.axis_index(Q)
    for i in range(weights.shape[0]):
        expert = (z ^ (i // 2)) * 2 + (x ^ (i % 2))
        weights[i : i + 1, :] = jnp.sum(jnp.where(routes[...] == expert, gates[...], 0.0), axis=0, keepdims=True)
    position = lax.broadcasted_iota(jnp.int32, (PLEN, live.shape[1]), 0)
    for p in range(live.shape[0] // PLEN):
        live[p * PLEN : (p + 1) * PLEN, :] = jnp.where(position < lengths[p], 0.0, -jnp.inf)
    count, span = chosen.shape[0] // 2, chosen.shape[0] // chosen.shape[1]
    query = lax.broadcasted_iota(jnp.int32, (count, chosen.shape[1]), 0) // span
    column = lax.broadcasted_iota(jnp.int32, (count, chosen.shape[1]), 1)
    for w in (0, 1):
        hit = jnp.where(column == query + (x ^ w) * (count // span), 1.0, 0.0)
        chosen[w * count : (w + 1) * count, :] = hit.astype(chosen.dtype)


def finish(act, tile, width):
    rows = act.shape[0] // 2
    gate_act, up_act = act[:rows], act[rows:]
    hidden = (gate_act / (1.0 + jnp.exp(-gate_act)) * up_act).astype(jnp.bfloat16)
    folded = jnp.concatenate([tile[:, i * width : (i + 1) * width] for i in range(rows // FOLD)], axis=0)
    return dot(folded, hidden, TN)


def through(x, cores, width):
    total = None
    for blocks, fold in cores:
        part = finish(dot(jnp.concatenate(blocks, axis=0), x, NT), fold, width)
        total = part if total is None else total + part
    return total


def own_cores(gate, up, fold, pair_gate, pair_up, pair_fold):
    return [([gate[...], up[...]], fold[...]), ([pair_gate[...], pair_up[...]], pair_fold[...])]


def other_cores(*refs):
    first = lax.axis_index(G) == 0
    cores = []
    for mine, others, rest_gate, rest_up in (refs[:4], refs[4:]):
        left = rest_gate.shape[0]
        gate, up = jnp.where(first, mine[...], others[...]), jnp.where(first, others[...], mine[...])
        cores.append(([gate, rest_gate[...], up, rest_up[:left, :]], rest_up[left:, :]))
    return cores


def at_end():
    z = lax.axis_index(E)
    return (z == 0) | (z == lax.axis_size(E) - 1)


def first_body(tokens, near, *refs):
    *own, got = refs
    x = jnp.concatenate([tokens[...], near[...]], axis=0)
    got[...] = through(x, own_cores(*own), got.shape[0])


def two_body(end_two, far_inner, *refs):
    *own, got = refs
    got[...] = through(jnp.where(at_end(), end_two[...], far_inner[...]), own_cores(*own), got.shape[0])


def second_body(tokens, near, end_two, far_inner, got_own, got_two, *refs):
    other, (here, back_near, back_two) = refs[:8], refs[8:]
    n, width = tokens.shape[0], got_own.shape[0]
    two = jnp.where(at_end(), end_two[...], far_inner[...])
    got = through(jnp.concatenate([tokens[...], near[...], two], axis=0), other_cores(*other), width)
    mine = [got_own[:, :n], got_own[:, n:], got_two[...]]
    for k, to in enumerate((here, back_near, back_two)):
        to[:width, :] = mine[k].astype(to.dtype)
        to[width : 2 * width, :] = got[:, k * n : (k + 1) * n].astype(to.dtype)
        if k:
            to[2 * width :, :] = jnp.zeros((to.shape[0] - 2 * width, n), to.dtype)


def third_body(end_three, across, earlier, *refs):
    own, other, to = refs[:6], refs[6:14], refs[14]
    width = to.shape[0] // 2
    three = jnp.where(at_end(), end_three[...], across[...])
    to[:width, :] = through(three, own_cores(*own), width).astype(to.dtype)
    to[width:, :] = through(three, other_cores(*other), width).astype(to.dtype)


def score_body(base, here, near, two, three, weights, live, chosen, queries, others, scores):
    width, tokens = base.shape
    total = base[...]
    for k, sent in enumerate((here, near, two, three)):
        for w in (0, 1):
            part = sent[w * width : (w + 1) * width, :].astype(jnp.float32)
            total = total + weights[2 * k + w : 2 * k + w + 1, :] * part
    norm = jnp.sqrt(jnp.sum(total * total, axis=0, keepdims=True) + 1e-06)
    embedding = (total / norm).T.astype(jnp.bfloat16)
    best = [[] for _ in range(tokens // PLEN)]
    for block in (queries, others):
        raw = dot(embedding, block[...], NT) + live[:, :1]
        for p, found in enumerate(best):
            found.append(jnp.max(raw[p * PLEN : (p + 1) * PLEN], axis=0, keepdims=True))
    left = jnp.concatenate([jnp.concatenate(found, axis=1) for found in best], axis=0)
    thirds = []
    for _ in range(3):
        thirds.append(left.astype(jnp.bfloat16).astype(jnp.float32))
        left = left - thirds[-1]
    sums = dot(jnp.concatenate(thirds, axis=0).astype(jnp.bfloat16), chosen[...])
    count = scores.shape[0]
    scores[...] = sums[:count] + (sums[count : 2 * count] + sums[2 * count :])


def by_column(
    tokens, route_ids, gate_values, passage_lengths, gate_weight, up_weight, down_weight, proj_weight, queries
):
    n, model_width = tokens.shape
    hidden_part = gate_weight.shape[2]
    width = proj_weight.shape[1]
    swap = [(0, 1), (1, 0)]
    ends, middle = [(1, 0), (2, 3)], [(1, 2), (2, 1)]
    f32, bf16 = jnp.float32, jnp.bfloat16

    rows = queries.shape[0] * queries.shape[1]
    both, longer = (2 * width, n), (2 * width + FOLD, n)
    near = lax.ppermute(tokens, E, [(i, i ^ 1) for i in range(4)])
    across = lax.ppermute(tokens, E, middle)
    gate, up, down = gate_weight[0].T, up_weight[0].T, down_weight[0].T
    part_rows = hidden_part // 2 // 16 * 16
    left = hidden_part - part_rows
    (part,) = kernel(part_body, [gate, up], [((part_rows, model_width), bf16)])
    part_x = lax.ppermute(part, Q, swap)
    fold, rest_gate, rest_up, held_gate, held_up, base, weights, live, chosen = kernel(
        fold_body,
        [passage_lengths, tokens, gate, up, down, proj_weight, route_ids.T, gate_values.T],
        [((r, model_width), bf16) for r in (FOLD, left, left + FOLD, hidden_part, hidden_part)]
        + [((width, n), f32), ((8, n), f32), ((n, width), f32), ((2 * rows, 2 * queries.shape[0]), bf16)],
        smem=(0,),
        fetched=(1,),
    )
    pair_gate, pair_up = lax.ppermute(gate, D, swap), lax.ppermute(up, D, swap)
    pair_fold = lax.ppermute(tied([fold], [pair_gate], 1)[0], D, swap)
    own = [held_gate, held_up, fold, pair_gate, pair_up, pair_fold]
    (got_own,) = kernel(first_body, [tokens, near, *own], [((width, 2 * n), f32)], fetched=(0,))

    far_inner = lax.ppermute(near, E, middle)
    end_two = lax.ppermute(across, E, ends)
    rest_x = [lax.ppermute(a, Q, swap) for a in (*tied([rest_gate], [pair_gate, pair_up], 1), *tied([rest_up], [near, across], 1))]
    (part_x,) = tied([part_x], [near, across], 1)
    part_y = lax.ppermute(part_x, G, swap)
    (got_two,) = kernel(two_body, [end_two, far_inner, *own], [((width, n), f32)])

    end_three = lax.ppermute(far_inner, E, ends)
    other = [part_x, part_y, *rest_x]
    free = {i: lax.ppermute(other[i], D, swap) for i in (2,)}
    held = dict(zip((0, 1, 3), tied([other[i] for i in (0, 1, 3)], [far_inner, got_own, got_two, free[2]], 1)))
    other = other + [free[i] if i in free else lax.ppermute(held[i], D, swap) for i in range(4)]
    other_queries = lax.ppermute(queries, Q, swap)
    here, *back = kernel(
        second_body,
        [tokens, near, end_two, far_inner, got_own, got_two, *other],
        [(both, f32), (longer, bf16), (longer, bf16)],
        fetched=(0,),
    )
    back += kernel(third_body, [end_three, across, here, *own, *other], [(both, bf16)])
    from_near, two, three = (
        lax.ppermute(a, E, [(i, i ^ k) for i in range(4)]) for k, a in enumerate(back, start=1)
    )
    (scores,) = kernel(
        score_body,
        [
            base, here, from_near, two, three, weights, live, chosen,
            queries.reshape(rows, width), other_queries.reshape(rows, width),
        ],
        [((n // PLEN, 2 * queries.shape[0]), f32)],
    )
    return scores


def solution(mesh):
    in_specs = (
        P((G, E, Q, D), None),
        P((G, E, Q, D), None),
        P((G, E, Q, D), None),
        P((G, E, Q, D)),
        P((E, Q), None, D),
        P((E, Q), None, D),
        P((E, Q), None, D),
        P(),
        P((G, Q), None, None),
    )
    sizes = [mesh.shape[a] for a in (G, E, Q, D)]
    return jax.shard_map(
        by_column if sizes == [2, 4, 2, 2] else by_dispatch,
        mesh=mesh,
        in_specs=in_specs,
        out_specs=P((G, E, Q, D), None),
        check_vma=False,
    )
```

```python
import jax
import jax.numpy as jnp
from jax import lax
from jax.experimental import pallas as pl
from jax.experimental.pallas import tpu as pltpu
from jax.sharding import PartitionSpec as P

PLEN = 64
G, E, Q, D = "group", "expert", "query", "dp"


def matched(embedding, live_mask, block_queries):
    query_rows = block_queries.reshape(-1, block_queries.shape[-1])
    raw_scores = jnp.dot(embedding, query_rows.T, preferred_element_type=jnp.float32)
    raw_scores = jnp.where(live_mask[:, None], raw_scores, -jnp.inf)
    best_match = jnp.max(raw_scores.reshape(-1, PLEN, raw_scores.shape[-1]), axis=1)
    return jnp.sum(best_match.reshape(best_match.shape[0], -1, block_queries.shape[1]), axis=-1)


def embedded(projected):
    lengths_norm = jnp.sqrt(jnp.sum(projected * projected, axis=-1, keepdims=True) + 1e-06)
    return (projected / lengths_norm).astype(jnp.bfloat16)


def live_tokens(passage_lengths, tok_rows):
    position = jnp.arange(tok_rows, dtype=jnp.int32) % PLEN
    return position < jnp.repeat(passage_lengths, PLEN)


def by_dispatch(
    tokens, route_ids, gate_values, passage_lengths, gate_weight, up_weight, down_weight, proj_weight, queries
):
    tok_rows, model_width = tokens.shape
    top_count = route_ids.shape[1]
    experts = lax.axis_size(E) * lax.axis_size(Q)
    capacity = max(2, 2 * tok_rows * top_count // experts)
    assignments = tok_rows * top_count
    flat_routes = route_ids.reshape(-1)
    one_hot = flat_routes[:, None] == jnp.arange(experts, dtype=jnp.int32)[None, :]
    order = jnp.arange(assignments, dtype=jnp.int32)
    before = (order[None, :] < order[:, None]).astype(jnp.bfloat16)
    earlier = jnp.dot(before, one_hot.astype(jnp.bfloat16), preferred_element_type=jnp.float32)
    slot_index = jnp.sum(jnp.where(one_hot, earlier, 0.0), axis=1).astype(jnp.int32)
    slot_target = flat_routes * capacity + slot_index
    slot_owner = jnp.full((experts * capacity,), assignments, jnp.int32).at[slot_target].set(order)
    padded = jnp.concatenate([tokens, jnp.zeros((1, model_width), tokens.dtype)], axis=0)
    source_row = jnp.where(slot_owner < assignments, slot_owner // top_count, tok_rows)
    outgoing = padded[source_row].reshape(experts, capacity, model_width)
    arrived = lax.all_to_all(outgoing, (E, Q), split_axis=0, concat_axis=0, tiled=True)
    expert_rows = arrived.reshape(experts * capacity, model_width)
    gate_act = jnp.dot(
        expert_rows, lax.all_gather(gate_weight[0], D, axis=1, tiled=True), preferred_element_type=jnp.float32
    )
    up_act = jnp.dot(
        expert_rows, lax.all_gather(up_weight[0], D, axis=1, tiled=True), preferred_element_type=jnp.float32
    )
    hidden = (jax.nn.silu(gate_act) * up_act).astype(jnp.bfloat16)
    results = lax.dot_general(
        hidden,
        lax.all_gather(down_weight[0], D, axis=1, tiled=True),
        (((1,), (1,)), ((), ())),
        preferred_element_type=jnp.float32,
    ).astype(jnp.bfloat16)
    folded = jnp.dot(results, proj_weight, preferred_element_type=jnp.float32)
    returned_rows = lax.all_to_all(
        folded.reshape(experts, capacity, folded.shape[-1]), (E, Q), split_axis=0, concat_axis=0, tiled=True
    )
    picked = returned_rows.reshape(experts * capacity, folded.shape[-1])[slot_target]
    weights = gate_values.reshape(assignments, 1)
    projected = jnp.dot(tokens, proj_weight, preferred_element_type=jnp.float32) + jnp.sum(
        (picked * weights).reshape(tok_rows, top_count, folded.shape[-1]), axis=1
    )
    live_mask = live_tokens(passage_lengths, tok_rows)
    return matched(embedded(projected), live_mask, lax.all_gather(queries, Q, axis=0, tiled=True))


VMEM = pl.BlockSpec(memory_space=pltpu.VMEM)
SMEM = pl.BlockSpec(memory_space=pltpu.SMEM)
NT, TN = (((1,), (1,)), ((), ())), (((0,), (0,)), ((), ()))


def dot(a, b, dims=(((1,), (0,)), ((), ()))):
    return lax.dot_general(a, b, dims, preferred_element_type=jnp.float32)


def whole_block(a):
    return pl.BlockSpec(a.shape, lambda *_: (0,) * a.ndim)


def tied(values, after, parts):
    def body(*refs):
        outs = refs[len(values) + len(after) :]
        for i in range(len(values)):
            rows = outs[parts * i].shape[0]
            for p in range(parts):
                outs[parts * i + p][...] = refs[i][p * rows : (p + 1) * rows, :]

    blocks = [jax.ShapeDtypeStruct((a.shape[0] // parts, a.shape[1]), a.dtype) for a in values for _ in range(parts)]

    return pl.pallas_call(
        body,
        out_shape=blocks,
        in_specs=[VMEM] * len(values) + [pl.BlockSpec(memory_space=pl.ANY)] * len(after),
        out_specs=[VMEM] * len(blocks),
        compiler_params=pltpu.CompilerParams(vmem_limit_bytes=8 * 2**20),
    )(*values, *after)


def kernel(body, operands, outs, smem=(), fetched=(), limit=24, flops=0):
    return pl.pallas_call(
        body,
        out_shape=[jax.ShapeDtypeStruct(shape, dtype) for shape, dtype in outs],
        in_specs=[
            SMEM if i in smem else whole_block(a) if i in fetched else VMEM for i, a in enumerate(operands)
        ],
        out_specs=[VMEM] * len(outs),
        compiler_params=pltpu.CompilerParams(vmem_limit_bytes=limit * 2**20),
        cost_estimate=pl.CostEstimate(flops=flops, bytes_accessed=0, transcendentals=0),
    )(*operands)


FOLD = 16


def part_body(gate, up, part):
    rows = part.shape[0]
    part[...] = jnp.where(lax.axis_index(G) == 0, gate[:rows, :], up[:rows, :])


def fold_body(
    lengths, tokens, gate, up, down, proj, routes, gates,
    fold, rest_gate, rest_up, held_gate, held_up, base, weights, live, chosen,
):
    rows, width = down.shape[0], proj.shape[1]
    folded = dot(down[...], proj[...]).astype(jnp.bfloat16)
    fold[...] = jnp.zeros_like(fold)
    for i in range(rows // FOLD):
        fold[:, i * width : (i + 1) * width] = folded[i * FOLD : (i + 1) * FOLD]
    left = rest_gate.shape[0]
    rest_gate[...] = gate[rows - left :, :]
    rest_up[:left, :] = up[rows - left :, :]
    rest_up[left:, :] = fold[...]
    held_gate[...] = gate[...]
    held_up[...] = up[...]
    base[...] = dot(tokens[...], proj[...]).T
    z, x = lax.axis_index(E), lax.axis_index(Q)
    for i in range(weights.shape[0]):
        expert = (z ^ (i // 2)) * 2 + (x ^ (i % 2))
        weights[i : i + 1, :] = jnp.sum(jnp.where(routes[...] == expert, gates[...], 0.0), axis=0, keepdims=True)
    position = lax.broadcasted_iota(jnp.int32, (PLEN, live.shape[1]), 0)
    for p in range(live.shape[0] // PLEN):
        live[p * PLEN : (p + 1) * PLEN, :] = jnp.where(position < lengths[p], 0.0, -jnp.inf)
    count, span = chosen.shape[0] // 2, chosen.shape[0] // chosen.shape[1]
    query = lax.broadcasted_iota(jnp.int32, (count, chosen.shape[1]), 0) // span
    column = lax.broadcasted_iota(jnp.int32, (count, chosen.shape[1]), 1)
    for w in (0, 1):
        hit = jnp.where(column == query + (x ^ w) * (count // span), 1.0, 0.0)
        chosen[w * count : (w + 1) * count, :] = hit.astype(chosen.dtype)


def finish(act, tile, width):
    rows = act.shape[0] // 2
    gate_act, up_act = act[:rows], act[rows:]
    hidden = (gate_act / (1.0 + jnp.exp(-gate_act)) * up_act).astype(jnp.bfloat16)
    folded = jnp.concatenate([tile[:, i * width : (i + 1) * width] for i in range(rows // FOLD)], axis=0)
    return dot(folded, hidden, TN)


def through(x, cores, width):
    total = None
    for blocks, fold in cores:
        part = finish(dot(jnp.concatenate(blocks, axis=0), x, NT), fold, width)
        total = part if total is None else total + part
    return total


def own_cores(gate, up, fold, pair_gate, pair_up, pair_fold):
    return [([gate[...], up[...]], fold[...]), ([pair_gate[...], pair_up[...]], pair_fold[...])]


def other_cores(*refs):
    first = lax.axis_index(G) == 0
    cores = []
    for mine, others, rest_gate, rest_up in (refs[:4], refs[4:]):
        left = rest_gate.shape[0]
        gate, up = jnp.where(first, mine[...], others[...]), jnp.where(first, others[...], mine[...])
        cores.append(([gate, rest_gate[...], up, rest_up[:left, :]], rest_up[left:, :]))
    return cores


def at_end():
    z = lax.axis_index(E)
    return (z == 0) | (z == lax.axis_size(E) - 1)


def first_body(tokens, near, *refs):
    *own, got = refs
    x = jnp.concatenate([tokens[...], near[...]], axis=0)
    got[...] = through(x, own_cores(*own), got.shape[0])


def two_body(end_two, far_inner, *refs):
    *own, got = refs
    got[...] = through(jnp.where(at_end(), end_two[...], far_inner[...]), own_cores(*own), got.shape[0])


def second_body(tokens, near, end_two, far_inner, got_own, got_two, *refs):
    other, (here, back_near, back_two) = refs[:8], refs[8:]
    n, width = tokens.shape[0], got_own.shape[0]
    two = jnp.where(at_end(), end_two[...], far_inner[...])
    got = through(jnp.concatenate([tokens[...], near[...], two], axis=0), other_cores(*other), width)
    mine = [got_own[:, :n], got_own[:, n:], got_two[...]]
    for k, to in enumerate((here, back_near, back_two)):
        to[:width, :] = mine[k].astype(to.dtype)
        to[width : 2 * width, :] = got[:, k * n : (k + 1) * n].astype(to.dtype)
        if k:
            to[2 * width :, :] = jnp.zeros((to.shape[0] - 2 * width, n), to.dtype)


def third_body(end_three, across, earlier, *refs):
    own, other, to = refs[:6], refs[6:14], refs[14]
    width = to.shape[0] // 2
    three = jnp.where(at_end(), end_three[...], across[...])
    to[:width, :] = through(three, own_cores(*own), width).astype(to.dtype)
    to[width:, :] = through(three, other_cores(*other), width).astype(to.dtype)


def score_body(base, here, near, two, three, weights, live, chosen, queries, others, scores):
    width, tokens = base.shape
    total = base[...]
    for k, sent in enumerate((here, near, two, three)):
        for w in (0, 1):
            part = sent[w * width : (w + 1) * width, :].astype(jnp.float32)
            total = total + weights[2 * k + w : 2 * k + w + 1, :] * part
    scale = lax.rsqrt(jnp.sum(total * total, axis=0, keepdims=True) + 1e-06)
    embedding = (total * scale).T.astype(jnp.bfloat16)
    best = [[] for _ in range(tokens // PLEN)]
    for block in (queries, others):
        raw = dot(embedding, block[...], NT) + live[:, :1]
        for p, found in enumerate(best):
            found.append(jnp.max(raw[p * PLEN : (p + 1) * PLEN], axis=0, keepdims=True))
    left = jnp.concatenate([jnp.concatenate(found, axis=1) for found in best], axis=0)
    thirds = []
    for _ in range(3):
        thirds.append(left.astype(jnp.bfloat16).astype(jnp.float32))
        left = left - thirds[-1]
    sums = dot(jnp.concatenate(thirds, axis=0).astype(jnp.bfloat16), chosen[...])
    count = scores.shape[0]
    scores[...] = sums[:count] + (sums[count : 2 * count] + sums[2 * count :])


def by_column(
    tokens, route_ids, gate_values, passage_lengths, gate_weight, up_weight, down_weight, proj_weight, queries
):
    n, model_width = tokens.shape
    hidden_part = gate_weight.shape[2]
    width = proj_weight.shape[1]
    swap = [(0, 1), (1, 0)]
    ends, middle = [(1, 0), (2, 3)], [(1, 2), (2, 1)]
    f32, bf16 = jnp.float32, jnp.bfloat16

    rows = queries.shape[0] * queries.shape[1]
    both, longer = (2 * width, n), (2 * width + FOLD, n)
    near = lax.ppermute(tokens, E, [(i, i ^ 1) for i in range(4)])
    across = lax.ppermute(tokens, E, middle)
    gate, up, down = gate_weight[0].T, up_weight[0].T, down_weight[0].T
    part_rows = hidden_part // 2 // 16 * 16
    left = hidden_part - part_rows
    (part,) = kernel(part_body, [gate, up], [((part_rows, model_width), bf16)])
    part_x = lax.ppermute(part, Q, swap)
    fold, rest_gate, rest_up, held_gate, held_up, base, weights, live, chosen = kernel(
        fold_body,
        [passage_lengths, tokens, gate, up, down, proj_weight, route_ids.T, gate_values.T],
        [((r, model_width), bf16) for r in (FOLD, left, left + FOLD, hidden_part, hidden_part)]
        + [((width, n), f32), ((8, n), f32), ((n, width), f32), ((2 * rows, 2 * queries.shape[0]), bf16)],
        smem=(0,),
        fetched=(1,),
    )
    pair_gate, pair_up = lax.ppermute(gate, D, swap), lax.ppermute(up, D, swap)
    pair_fold = lax.ppermute(tied([fold], [pair_gate], 1)[0], D, swap)
    own = [held_gate, held_up, fold, pair_gate, pair_up, pair_fold]
    (got_own,) = kernel(first_body, [tokens, near, *own], [((width, 2 * n), f32)], fetched=(0,))

    far_inner = lax.ppermute(near, E, middle)
    end_two = lax.ppermute(across, E, ends)
    rest_x = [lax.ppermute(a, Q, swap) for a in (*tied([rest_gate], [pair_gate, pair_up], 1), *tied([rest_up], [near, across], 1))]
    (part_x,) = tied([part_x], [near, across], 1)
    part_y = lax.ppermute(part_x, G, swap)
    (got_two,) = kernel(two_body, [end_two, far_inner, *own], [((width, n), f32)])

    end_three = lax.ppermute(far_inner, E, ends)
    other = [part_x, part_y, *rest_x]
    free = {i: lax.ppermute(other[i], D, swap) for i in (2,)}
    held = dict(zip((0, 1, 3), tied([other[i] for i in (0, 1, 3)], [far_inner, got_own, got_two, free[2]], 1)))
    other = other + [free[i] if i in free else lax.ppermute(held[i], D, swap) for i in range(4)]
    other_queries = lax.ppermute(queries, Q, swap)
    here, *back = kernel(
        second_body,
        [tokens, near, end_two, far_inner, got_own, got_two, *other],
        [(both, f32), (longer, bf16), (longer, bf16)],
        fetched=(0,),
    )
    back += kernel(third_body, [end_three, across, here, *own, *other], [(both, bf16)])
    from_near, two, three = (
        lax.ppermute(a, E, [(i, i ^ k) for i in range(4)]) for k, a in enumerate(back, start=1)
    )
    (scores,) = kernel(
        score_body,
        [
            base, here, from_near, two, three, weights, live, chosen,
            queries.reshape(rows, width), other_queries.reshape(rows, width),
        ],
        [((n // PLEN, 2 * queries.shape[0]), f32)],
    )
    return scores


def solution(mesh):
    in_specs = (
        P((G, E, Q, D), None),
        P((G, E, Q, D), None),
        P((G, E, Q, D), None),
        P((G, E, Q, D)),
        P((E, Q), None, D),
        P((E, Q), None, D),
        P((E, Q), None, D),
        P(),
        P((G, Q), None, None),
    )
    sizes = [mesh.shape[a] for a in (G, E, Q, D)]
    return jax.shard_map(
        by_column if sizes == [2, 4, 2, 2] else by_dispatch,
        mesh=mesh,
        in_specs=in_specs,
        out_specs=P((G, E, Q, D), None),
        check_vma=False,
    )
```
